32 devices in a mesh: samp: 4 (over x, core), pair: 8 (over z, y).
Axes of the slice: x: 2, y: 2, z: 4, core: 2. Of those that a mesh axis runs over, the one named last changes fastest.
Arguments:
- matrix: bfloat16 [32768, 4096], P('samp', 'pair'), may hold values from -48 to 48
- tournament: int32 [2, 8], replicated, may hold values from 0 to 1
Outputs:
- result: bfloat16 [32768, 4096], P('samp', 'pair')
The draws below stay inside these ranges and needn't reach their ends.
All inputs are finite; a program needn't handle non-finite values.
Results may differ from the reference program's by a relative error of at most 0.008.
Values may be sent and summed in bfloat16 or wider, within the bound.
No kernel may reach another device: no remote copies, remote signals or barrier semaphores. Data moves between devices by JAX's collectives and lax.ppermute only.
A program may use at most 128 MiB of HBM per device.

```python
import math
import jax
import jax.numpy as jnp
from jax import lax

BLOCK_COLS = 256
ROUNDS = 2
POLAR_STEPS = 5
SAMPLES = 32768
COLUMNS = 4096


def draw_matrix(key, part):
    sample_pos = jnp.arange(SAMPLES, dtype=jnp.float32)
    sample_ramp = jnp.exp(0.55 * sample_pos / SAMPLES)
    jitter = jnp.exp(jax.random.uniform(jax.random.fold_in(key, 1), (SAMPLES,), jnp.float32, math.log(0.5), math.log(3.0)))
    column_scale = jnp.exp(jax.random.uniform(jax.random.fold_in(key, 2), (COLUMNS,), jnp.float32, math.log(0.4), math.log(4.0)))
    base_values = jnp.clip(jax.random.normal(jax.random.fold_in(key, 3), (SAMPLES, COLUMNS), jnp.float32), -4.0, 4.0)
    return (0.5 * base_values * (sample_ramp * jitter)[:, None] * column_scale[None, :]).astype(jnp.bfloat16)


def place_ends(array, own_key, least, top_value):
    longest = array.shape.index(max(array.shape))
    spots = []
    for shift in (0, 1):
        where = [jax.random.randint(jax.random.fold_in(own_key, axis), (), 0, length) for axis, length in enumerate(array.shape)]
        where[longest] = (where[longest] + shift) % array.shape[longest]
        spots.append(tuple(where))
    return array.at[spots[0]].set(least).at[spots[1]].set(top_value)


def setup_inputs(seed: int = 0) -> dict:
    splits = jax.random.split(jax.random.key(seed), 3)
    matrix = draw_matrix(jax.random.fold_in(splits[2], 71), 0)
    tournament = place_ends(jax.random.randint(splits[1], (ROUNDS, COLUMNS // (2 * BLOCK_COLS)), 0, 2), jax.random.fold_in(splits[1], 1), 0, 1).astype(jnp.int32)
    return dict(matrix=matrix, tournament=tournament)


coupling = 2.0
start_scale = 6.0

def polar_rotation(cross_gram):
    block_width = cross_gram.shape[0]
    frobenius = jnp.sqrt(jnp.sum(cross_gram * cross_gram) + 1e-06)
    coupled = coupling * cross_gram / frobenius
    blank_block = jnp.zeros_like(coupled)
    skew_matrix = jnp.concatenate([jnp.concatenate([blank_block, -coupled], 1), jnp.concatenate([coupled.T, blank_block], 1)], 0)
    iterate = (jnp.eye(2 * block_width, dtype=coupled.dtype) + skew_matrix) / start_scale
    for iteration in range(POLAR_STEPS):
        rounded = iterate.astype(jnp.bfloat16)
        square = lax.dot_general(rounded, rounded, (((0,), (0,)), ((), ())), preferred_element_type=jnp.float32).astype(jnp.bfloat16)
        iterate = 1.5 * iterate - 0.5 * jnp.dot(rounded, square, preferred_element_type=jnp.float32)
    return iterate.astype(jnp.bfloat16)

def slot_round(inputs):
    current, selector = inputs
    block_width = current.shape[1] // 2
    cross_gram = lax.dot_general(current[:, :block_width], current[:, block_width:], (((0,), (0,)), ((), ())), preferred_element_type=jnp.float32)
    rotation = polar_rotation(cross_gram)
    rotated = jnp.dot(current, rotation, preferred_element_type=jnp.float32).astype(jnp.bfloat16)
    first_half = rotated[:, :block_width]
    second_half = rotated[:, block_width:]
    kept_block = jnp.where(selector == 1, second_half, first_half)
    moving_block = jnp.where(selector == 1, first_half, second_half)
    return (kept_block, moving_block)

def reference(matrix, tournament):
    slot_count = COLUMNS // (2 * BLOCK_COLS)
    blocks = matrix.reshape(SAMPLES, slot_count, 2 * BLOCK_COLS).transpose(1, 0, 2)
    for tourney in range(ROUNDS):
        kept_block, moving_block = lax.map(slot_round, (blocks, tournament[tourney]))
        blocks = jnp.concatenate([jnp.roll(kept_block, -(slot_count // 2), axis=0), jnp.roll(moving_block, 1, axis=0)], axis=2)
    return blocks.transpose(1, 0, 2).reshape(SAMPLES, COLUMNS)
```

```python
import jax
import jax.numpy as jnp
from jax import lax
from jax.sharding import PartitionSpec as P

ROUNDS = 2
POLAR_STEPS = 5
CHUNKS = 4


coupling = 2.0
start_scale = 6.0


def polar_rotation(cross_gram):
    block_width = cross_gram.shape[0]
    frobenius = jnp.sqrt(jnp.sum(cross_gram * cross_gram) + 1e-06)
    coupled = coupling * cross_gram / frobenius
    blank_block = jnp.zeros_like(coupled)
    skew_matrix = jnp.concatenate(
        [jnp.concatenate([blank_block, -coupled], 1), jnp.concatenate([coupled.T, blank_block], 1)],
        0,
    )
    iterate = (jnp.eye(2 * block_width, dtype=coupled.dtype) + skew_matrix) / start_scale
    for iteration in range(POLAR_STEPS):
        rounded = iterate.astype(jnp.bfloat16)
        square = lax.dot_general(
            rounded, rounded, (((0,), (0,)), ((), ())), preferred_element_type=jnp.float32
        ).astype(jnp.bfloat16)
        iterate = 1.5 * iterate - 0.5 * jnp.dot(rounded, square, preferred_element_type=jnp.float32)
    return iterate.astype(jnp.bfloat16)


def summed(value):
    length = lax.axis_size("samp")
    if length & (length - 1):
        return lax.psum(value.astype(jnp.bfloat16), "samp").astype(jnp.float32)
    total = value.astype(jnp.bfloat16)
    step = 1
    while step < length:
        other = lax.ppermute(total, "samp", [(i, i ^ step) for i in range(length)])
        total = total.astype(jnp.float32) + other.astype(jnp.float32)
        step *= 2
        if step < length:
            total = total.astype(jnp.bfloat16)
    return total.astype(jnp.float32)


def cross(first, second):
    return lax.dot_general(
        first, second, (((0,), (0,)), ((), ())), preferred_element_type=jnp.float32
    )


def shards(matrix, tournament):
    cycle_size = lax.axis_size("pair")
    half_cycle = cycle_size // 2
    position = lax.axis_index("pair")
    odd = position % 2 == 1
    rows, width = matrix.shape[0], matrix.shape[1] // 2
    piece = rows // CHUNKS

    def target(p):
        return (p + half_cycle + 1) % cycle_size

    everyone = [(p, target(p)) for p in range(cycle_size)]
    from_odd = [(p, target(p)) for p in range(1, cycle_size, 2)]
    to_neighbour = [(p, p + 1) for p in range(0, cycle_size, 2)]
    forward = [(p + 1, target(p)) for p in range(0, cycle_size, 2)]

    kept, arrived = matrix[:, :width], [matrix[i * piece : (i + 1) * piece, width:] for i in range(CHUNKS)]
    for tourney in range(ROUNDS):
        slot_index = (position + half_cycle * (tourney % 2)) % cycle_size
        selector = tournament[tourney, slot_index]
        if tourney == 0:
            gram = cross(matrix[:, :width], matrix[:, width:])
            parts = [matrix[i * piece : (i + 1) * piece] for i in range(CHUNKS)]
        else:
            parts = [
                jnp.concatenate([kept[i * piece : (i + 1) * piece], arrived[i]], axis=1)
                for i in range(CHUNKS)
            ]
            gram = sum(cross(kept[i * piece : (i + 1) * piece], arrived[i]) for i in range(CHUNKS))
        rotation = polar_rotation(summed(gram))
        first_cols = rotation[:, :width]
        second_cols = rotation[:, width:]
        keep_columns = jnp.where(selector == 1, second_cols, first_cols)
        move_columns = jnp.where(selector == 1, first_cols, second_cols)

        def times(part, columns):
            return jnp.dot(part, columns, preferred_element_type=jnp.float32).astype(jnp.bfloat16)

        last = times(parts[-1], move_columns)
        passed = lax.ppermute(last, "pair", to_neighbour)
        got = [lax.ppermute(times(part, move_columns), "pair", everyone) for part in parts[:-1]]
        own = lax.ppermute(last, "pair", from_odd)
        kept = jnp.concatenate([times(part, keep_columns) for part in parts], axis=0)
        far = lax.ppermute(passed, "pair", forward)
        arrived = got + [jnp.where(odd, far, own)]
    return jnp.concatenate([kept, jnp.concatenate(arrived, axis=0)], axis=1)


def solution(mesh):
    placed = (P("samp", "pair"), P())
    return jax.shard_map(
        shards, mesh=mesh, in_specs=placed, out_specs=P("samp", "pair"), check_vma=False
    )
```

```python
import functools

import jax
import jax.numpy as jnp
from jax import lax
from jax.experimental import pallas as pl
from jax.experimental.pallas import tpu as pltpu
from jax.sharding import PartitionSpec as P

ROUNDS = 2
POLAR_STEPS = 5
CHUNKS = 4
TILE = 1024
VMEM_LIMIT = 32 * 1024 * 1024


coupling = 2.0
start_scale = 6.0


def rotation_kernel(selector, mine, other, moving, keeping, iterate):
    width = mine.shape[0]
    gram = mine[...].astype(jnp.float32) + other[...].astype(jnp.float32)
    frobenius = jnp.sqrt(jnp.sum(gram * gram, keepdims=True) + 1e-06)
    coupled = coupling * gram / frobenius
    row = lax.broadcasted_iota(jnp.int32, (width, width), 0)
    column = lax.broadcasted_iota(jnp.int32, (width, width), 1)
    diagonal = (row == column).astype(jnp.float32) / start_scale
    iterate[:width, :width] = diagonal
    iterate[width:, width:] = diagonal
    iterate[:width, width:] = -coupled / start_scale
    iterate[width:, :width] = coupled.T / start_scale

    def step(_, carry):
        current = iterate[...]
        rounded = current.astype(jnp.bfloat16)
        square = lax.dot_general(
            rounded, rounded, (((0,), (0,)), ((), ())), preferred_element_type=jnp.float32
        ).astype(jnp.bfloat16)
        iterate[...] = 1.5 * current - 0.5 * jnp.dot(
            rounded, square, preferred_element_type=jnp.float32
        )
        return carry

    lax.fori_loop(0, POLAR_STEPS, step, 0)
    first = iterate[:, :width].astype(jnp.bfloat16)
    second = iterate[:, width:].astype(jnp.bfloat16)
    second_stays = selector[0] == 1

    @pl.when(second_stays)
    def _():
        moving[...] = first
        keeping[...] = second

    @pl.when(jnp.logical_not(second_stays))
    def _():
        moving[...] = second
        keeping[...] = first


def rotation_columns(selector, mine, other):
    width = mine.shape[0]
    columns = jax.ShapeDtypeStruct((2 * width, width), jnp.bfloat16)
    vmem = pl.BlockSpec(memory_space=pltpu.VMEM)
    return pl.pallas_call(
        rotation_kernel,
        out_shape=(columns, columns),
        in_specs=[pl.BlockSpec(memory_space=pltpu.SMEM), vmem, vmem],
        out_specs=(vmem, vmem),
        scratch_shapes=[pltpu.VMEM((2 * width, 2 * width), jnp.float32)],
        compiler_params=pltpu.CompilerParams(vmem_limit_bytes=VMEM_LIMIT),
        cost_estimate=pl.CostEstimate(
            flops=2 * 2 * POLAR_STEPS * (2 * width) ** 3, bytes_accessed=10 * width**2, transcendentals=0
        ),
    )(selector, mine, other)


def place_rotated_kernel(kept, arrived, columns, *rest):
    out = rest[-1]
    width = kept.shape[1]
    out[...] = (
        jnp.dot(kept[...], columns[:width], preferred_element_type=jnp.float32)
        + jnp.dot(arrived[...], columns[width:], preferred_element_type=jnp.float32)
    ).astype(out.dtype)


def place_rotated(kept, arrived, columns, out, chunk):
    rows, width = arrived.shape
    tile = min(TILE, rows)
    first = chunk * (rows // tile)
    before = [] if out is None else [out]
    return pl.pallas_call(
        place_rotated_kernel,
        grid=(rows // tile,),
        out_shape=jax.ShapeDtypeStruct((kept.shape[0], 2 * width), kept.dtype),
        in_specs=[
            pl.BlockSpec((tile, width), lambda i: (i + first, 0)),
            pl.BlockSpec((tile, width), lambda i: (i, 0)),
            pl.BlockSpec((2 * width, width), lambda i: (0, 0)),
        ]
        + [pl.BlockSpec(memory_space=pl.ANY)] * len(before),
        out_specs=pl.BlockSpec((tile, width), lambda i: (i + first, 0)),
        input_output_aliases={3: 0} if before else {},
        compiler_params=pltpu.CompilerParams(vmem_limit_bytes=VMEM_LIMIT),
        cost_estimate=pl.CostEstimate(
            flops=4 * rows * width**2, bytes_accessed=6 * rows * width, transcendentals=0
        ),
    )(kept, arrived, columns, *before)


def place_kernel(block, _, out):
    out[...] = block[...]


def place_either_kernel(pick, one, other, _, out):
    out[...] = jnp.where(pick[0] == 1, one[...], other[...])


def place(blocks, out, chunk, pick=None):
    rows, width = blocks[0].shape
    tile = min(TILE, rows)
    first = chunk * (rows // tile)
    block = pl.BlockSpec((tile, width), lambda i: (i, 0))
    ahead = [] if pick is None else [pick]
    return pl.pallas_call(
        place_kernel if pick is None else place_either_kernel,
        grid=(rows // tile,),
        out_shape=jax.ShapeDtypeStruct(out.shape, out.dtype),
        in_specs=[pl.BlockSpec(memory_space=pltpu.SMEM)] * len(ahead)
        + [block] * len(blocks)
        + [pl.BlockSpec(memory_space=pl.ANY)],
        out_specs=pl.BlockSpec((tile, width), lambda i: (i + first, 1)),
        input_output_aliases={len(ahead) + len(blocks): 0},
        compiler_params=pltpu.CompilerParams(vmem_limit_bytes=VMEM_LIMIT),
        cost_estimate=pl.CostEstimate(flops=0, bytes_accessed=4 * rows * width, transcendentals=0),
    )(*ahead, *blocks, out)


def summed(value):
    length = lax.axis_size("samp")
    total = value.astype(jnp.bfloat16)
    if length & (length - 1):
        return lax.psum(total, "samp"), jnp.zeros_like(total)
    other = jnp.zeros_like(total)
    step = 1
    while step < length:
        if step > 1:
            total = (total.astype(jnp.float32) + other.astype(jnp.float32)).astype(jnp.bfloat16)
        other = lax.ppermute(total, "samp", [(i, i ^ step) for i in range(length)])
        step *= 2
    return total, other


def cross(first, second):
    return lax.dot_general(
        first, second, (((0,), (0,)), ((), ())), preferred_element_type=jnp.float32
    )


def shards(matrix, tournament):
    cycle_size = lax.axis_size("pair")
    half_cycle = cycle_size // 2
    position = lax.axis_index("pair")
    odd = (position % 2).astype(jnp.int32)
    rows, width = matrix.shape[0], matrix.shape[1] // 2
    piece = rows // CHUNKS

    def target(p):
        return (p + half_cycle + 1) % cycle_size

    def chunk_of(array, i):
        return array[i * piece : (i + 1) * piece]

    everyone = [(p, target(p)) for p in range(cycle_size)]
    from_odd = [(p, target(p)) for p in range(1, cycle_size, 2)]
    to_neighbour = [(p, p + 1) for p in range(0, cycle_size, 2)]
    forward = [(p + 1, target(p)) for p in range(0, cycle_size, 2)]

    def times(part, columns):
        return jnp.dot(part, columns, preferred_element_type=jnp.float32).astype(jnp.bfloat16)

    def sent(parts, columns):
        last = times(parts[-1], columns)
        passed = lax.ppermute(last, "pair", to_neighbour)
        got = [lax.ppermute(times(part, columns), "pair", everyone) for part in parts[:-1]]
        near = lax.ppermute(last, "pair", from_odd)
        far = lax.ppermute(passed, "pair", forward)
        return got, far, near

    def selector(tourney):
        slot_index = (position + half_cycle * (tourney % 2)) % cycle_size
        return lax.dynamic_slice(tournament[tourney], (slot_index,), (1,))

    moving, keeping = rotation_columns(selector(0), *summed(cross(matrix[:, :width], matrix[:, width:])))
    got, far, near = sent([chunk_of(matrix, i) for i in range(CHUNKS)], moving)
    kept = times(matrix, keeping)
    arrived = got + [jnp.where(odd == 1, far, near)]

    gram = sum(cross(chunk_of(kept, i), arrived[i]) for i in range(CHUNKS))
    moving, keeping = rotation_columns(selector(1), *summed(gram))
    parts = [jnp.concatenate([chunk_of(kept, i), arrived[i]], axis=1) for i in range(CHUNKS)]
    got, far, near = sent(parts, moving)
    out = None
    for i in range(CHUNKS):
        out = place_rotated(kept, arrived[i], keeping, out, i)
    for i in range(CHUNKS - 1):
        out = place([got[i]], out, i)
    return place([far, near], out, CHUNKS - 1, odd[None])


def solution(mesh):
    placed = (P("samp", "pair"), P())
    return jax.shard_map(
        shards, mesh=mesh, in_specs=placed, out_specs=P("samp", "pair"), check_vma=False
    )
```

```python
import functools

import jax
import jax.numpy as jnp
from jax import lax
from jax.experimental import pallas as pl
from jax.experimental.pallas import tpu as pltpu
from jax.sharding import PartitionSpec as P

POLAR_STEPS = 5
TILE = 1024
VMEM_LIMIT = 48 * 1024 * 1024


coupling = 2.0
start_scale = 6.0

IN_VMEM = pl.BlockSpec(memory_space=pltpu.VMEM)
IN_SMEM = pl.BlockSpec(memory_space=pltpu.SMEM)
ANYWHERE = pl.BlockSpec(memory_space=pl.ANY)
IN_HBM = pl.BlockSpec(memory_space=pltpu.MemorySpace.HBM)


def reads_of(t, sources, starts, tile, block, arrivals):
    rows = pl.multiple_of(t * tile, tile)
    copies, at = [], 0
    for s, (source, start) in enumerate(zip(sources, starts)):
        span = source.shape[1]
        copies.append(
            pltpu.make_async_copy(
                source.at[pl.ds(pl.multiple_of(start + rows, tile), tile)],
                block.at[pl.ds(rows, tile), pl.ds(at, span)],
                arrivals.at[s, t],
            )
        )
        at += span
    return copies


def start_reads(sources, starts, tiles, tile, block, arrivals):
    def start(t, carry):
        for copy in reads_of(t, sources, starts, tile, block, arrivals):
            copy.start()
        return carry

    lax.fori_loop(0, tiles, start, 0)


def write_rotated(sources, starts, tiles, tile, block, arrivals, columns, rotated, out, first_row, departures):
    def write_of(t):
        rows = pl.multiple_of(t * tile, tile)
        return pltpu.make_async_copy(
            rotated.at[pl.ds(rows, tile)],
            out.at[pl.ds(pl.multiple_of(first_row + rows, tile), tile), pl.ds(0, rotated.shape[1])],
            departures.at[t],
        )

    def rotate(t, carry):
        for copy in reads_of(t, sources, starts, tile, block, arrivals):
            copy.wait()
        here = pl.ds(pl.multiple_of(t * tile, tile), tile)
        rotated[here, :] = jnp.dot(
            block[here, :], columns[...], preferred_element_type=jnp.float32
        ).astype(rotated.dtype)
        write_of(t).start()
        return carry

    def finish(t, carry):
        write_of(t).wait()
        return carry

    lax.fori_loop(0, tiles, rotate, 0)
    lax.fori_loop(0, tiles, finish, 0)


def polar_columns(selector, mine, other, moving, keeping, iterate):
    width = mine.shape[0]
    gram = mine[...].astype(jnp.float32) + other[...].astype(jnp.float32)
    frobenius = jnp.sqrt(jnp.sum(gram * gram, keepdims=True) + 1e-06)
    coupled = coupling * gram / frobenius
    row = lax.broadcasted_iota(jnp.int32, (width, width), 0)
    column = lax.broadcasted_iota(jnp.int32, (width, width), 1)
    diagonal = (row == column).astype(jnp.float32) / start_scale
    iterate[:width, :width] = diagonal
    iterate[width:, width:] = diagonal
    iterate[:width, width:] = -coupled / start_scale
    iterate[width:, :width] = coupled.T / start_scale

    def step(_, carry):
        current = iterate[...]
        rounded = current.astype(jnp.bfloat16)
        square = lax.dot_general(
            rounded, rounded, (((0,), (0,)), ((), ())), preferred_element_type=jnp.float32
        ).astype(jnp.bfloat16)
        iterate[...] = 1.5 * current - 0.5 * jnp.dot(
            rounded, square, preferred_element_type=jnp.float32
        )
        return carry

    lax.fori_loop(0, POLAR_STEPS, step, 0)
    first = iterate[:, :width].astype(jnp.bfloat16)
    second = iterate[:, width:].astype(jnp.bfloat16)
    second_stays = selector[0] == 1

    @pl.when(second_stays)
    def _():
        moving[...] = first
        keeping[...] = second

    @pl.when(jnp.logical_not(second_stays))
    def _():
        moving[...] = second
        keeping[...] = first


def rotation_kernel(tile, starts_of, *refs):
    selector, mine, other = refs[:3]
    counts = [len(starts) for starts in starts_of]
    parts = len(counts)
    tail = refs[3 + sum(counts) :]
    moving, keeping = tail[:2]
    outs, iterate, block, rotated = tail[2 : 2 + parts], tail[2 + parts], tail[3 + parts], tail[4 + parts]
    arrivals, departures = tail[5 + parts :]
    rows = outs[0].shape[0]
    tiles = rows // tile
    at, pieces = 3, []
    for k, count in enumerate(counts):
        here = pl.ds(k * rows, rows)
        pieces.append(
            (refs[at : at + count], starts_of[k], tiles, tile, block.at[here], arrivals.at[k])
        )
        at += count
    for piece in pieces:
        start_reads(*piece)
    polar_columns(selector, mine, other, moving, keeping, iterate)
    for k, (sources, starts, _, _, rows_of, arrived) in enumerate(pieces):
        write_rotated(
            sources, starts, tiles, tile, rows_of, arrived, moving,
            rotated.at[pl.ds(k * rows, rows)], outs[k], 0, departures.at[k],
        )


def rotation_of(selector, terms, parts, starts_of, rows, where):
    width = terms[0].shape[0]
    tile = min(TILE, rows)
    counts = [len(part) for part in parts]
    columns = jax.ShapeDtypeStruct((2 * width, width), jnp.bfloat16)
    moved = jax.ShapeDtypeStruct((rows, width), jnp.bfloat16)
    return pl.pallas_call(
        functools.partial(rotation_kernel, tile, starts_of),
        out_shape=[columns, columns] + [moved] * len(parts),
        in_specs=[IN_SMEM, IN_VMEM, IN_VMEM] + where,
        out_specs=[IN_VMEM, IN_VMEM] + [IN_HBM] * len(parts),
        scratch_shapes=[
            pltpu.VMEM((2 * width, 2 * width), jnp.float32),
            pltpu.VMEM((len(parts) * rows, 2 * width), jnp.bfloat16),
            pltpu.VMEM((len(parts) * rows, width), jnp.bfloat16),
            pltpu.SemaphoreType.DMA((len(parts), max(counts), rows // tile)),
            pltpu.SemaphoreType.DMA((len(parts), rows // tile)),
        ],
        compiler_params=pltpu.CompilerParams(vmem_limit_bytes=VMEM_LIMIT),
        cost_estimate=pl.CostEstimate(
            flops=2 * 2 * POLAR_STEPS * (2 * width) ** 3 + 4 * len(parts) * rows * width**2,
            bytes_accessed=10 * width**2 + 6 * len(parts) * rows * width,
            transcendentals=0,
        ),
    )(selector, *terms, *[source for part in parts for source in part])


def rotated_kernel(starts, tile, rows, first_row, *refs):
    columns, sources = refs[0], refs[1 : 1 + len(starts)]
    out, block, rotated, arrivals, departures = refs[-5:]
    tiles = rows // tile
    start_reads(sources, starts, tiles, tile, block, arrivals)
    write_rotated(
        sources, starts, tiles, tile, block, arrivals, columns, rotated, out, first_row, departures
    )


def rotated_rows(sources, starts, rows, columns, where, shape=None, out=None, first_row=0):
    width = columns.shape[1]
    tile = min(TILE, rows)
    before = [] if out is None else [out]
    return pl.pallas_call(
        functools.partial(rotated_kernel, starts, tile, rows, first_row),
        out_shape=jax.ShapeDtypeStruct(shape or (rows, width), columns.dtype),
        in_specs=[IN_VMEM] + where + [IN_HBM] * len(before),
        out_specs=IN_HBM,
        input_output_aliases={1 + len(sources): 0} if before else {},
        scratch_shapes=[
            pltpu.VMEM((rows, 2 * width), jnp.bfloat16),
            pltpu.VMEM((rows, width), jnp.bfloat16),
            pltpu.SemaphoreType.DMA((len(sources), rows // tile)),
            pltpu.SemaphoreType.DMA((rows // tile,)),
        ],
        compiler_params=pltpu.CompilerParams(vmem_limit_bytes=VMEM_LIMIT),
        cost_estimate=pl.CostEstimate(
            flops=4 * rows * width**2, bytes_accessed=6 * rows * width, transcendentals=0
        ),
    )(columns, *sources, *before)


def place_kernel(tile, first_row, wanted, source, _, *refs):
    out, block, arrivals, departures = refs[-4:]
    rows, width = source.shape

    @pl.when(wanted[0] == 1)
    def _():
        reads = [
            pltpu.make_async_copy(
                source.at[pl.ds(t * tile, tile)], block.at[pl.ds(t * tile, tile)], arrivals.at[t]
            )
            for t in range(rows // tile)
        ]
        writes = [
            pltpu.make_async_copy(
                block.at[pl.ds(t * tile, tile)],
                out.at[pl.ds(first_row + t * tile, tile), pl.ds(width, width)],
                departures.at[t],
            )
            for t in range(rows // tile)
        ]
        for read in reads:
            read.start()
        for read, write in zip(reads, writes):
            read.wait()
            write.start()
        for write in writes:
            write.wait()


def place(wanted, source, out, first_row, after=()):
    rows, width = source.shape
    tile = min(TILE, rows)
    return pl.pallas_call(
        functools.partial(place_kernel, tile, first_row),
        out_shape=jax.ShapeDtypeStruct(out.shape, out.dtype),
        in_specs=[IN_SMEM, ANYWHERE, IN_HBM] + [ANYWHERE] * len(after),
        out_specs=IN_HBM,
        input_output_aliases={2: 0},
        scratch_shapes=[
            pltpu.VMEM((rows, width), jnp.bfloat16),
            pltpu.SemaphoreType.DMA((rows // tile,)),
            pltpu.SemaphoreType.DMA((rows // tile,)),
        ],
        compiler_params=pltpu.CompilerParams(vmem_limit_bytes=VMEM_LIMIT),
        cost_estimate=pl.CostEstimate(flops=0, bytes_accessed=4 * rows * width, transcendentals=0),
    )(wanted, source, out, *after)


def summed(value, positions):
    length, cycle_size = lax.axis_size("samp"), lax.axis_size("pair")
    total = value.astype(jnp.bfloat16)
    if length & (length - 1):
        return lax.psum(total, "samp"), jnp.zeros_like(total)
    other = jnp.zeros_like(total)
    step = 1
    while step < length:
        if step > 1:
            total = (total.astype(jnp.float32) + other.astype(jnp.float32)).astype(jnp.bfloat16)
        pairs = [(i * cycle_size + p, (i ^ step) * cycle_size + p) for i in range(length) for p in positions]
        other = lax.ppermute(total, ("samp", "pair"), pairs)
        step *= 2
    return total, other


def cross(first, second):
    return lax.dot_general(
        first, second, (((0,), (0,)), ((), ())), preferred_element_type=jnp.float32
    )


def shards(matrix, tournament):
    cycle_size = lax.axis_size("pair")
    half_cycle = cycle_size // 2
    position = lax.axis_index("pair")
    rows, width = matrix.shape[0], matrix.shape[1] // 2
    half = rows // 2

    def target(p):
        return (p + half_cycle + 1) % cycle_size

    def among(positions):
        found = sum((position == p).astype(jnp.int32) for p in positions)
        return found.reshape((1,))

    def passed(value, pairs):
        return lax.ppermute(value, "pair", pairs)

    def selector(tourney):
        slot_index = (position + half_cycle * (tourney % 2)) % cycle_size
        return lax.dynamic_slice(tournament[tourney], (slot_index,), (1,))

    def sends(positions):
        return [(p, target(p)) for p in positions]

    whole = list(range(cycle_size))
    late = [half_cycle - 1, cycle_size - 1]
    to_late = [p for p in whole if target(p) in late]
    others = [p for p in whole if p not in to_late]
    prompt = [p for p in whole if p not in late]
    late_ways = [
        (cycle_size - 2, half_cycle, cycle_size - 1, half_cycle - 1),
        (half_cycle - 2, half_cycle - 2, half_cycle - 1, cycle_size - 1),
    ]
    ways = [(0, half_cycle - 1, target(0)), (cycle_size - 2, half_cycle + 1, half_cycle - 1)]
    detoured = [source for source, _, _ in ways]
    straight = [p for p in prompt if p not in detoured]
    is_late = among(late)[0] == 1
    after_late = among([target(p) for p in late])
    after_detoured = among([target(p) for p in detoured])

    gram = cross(matrix[:, :width], matrix[:, width:])
    _, keeping, first, last = rotation_of(
        selector(0), summed(gram, whole), [[matrix], [matrix]], [[0], [half]], half, [IN_HBM] * 2
    )
    got_first = passed(first, sends(others))
    got_last = passed(last, sends(others))
    first = passed(first, [(source, by) for source, by, _, _ in late_ways])
    last = passed(last, [(source, by) for source, _, by, _ in late_ways])
    kept = rotated_rows([matrix], [0], rows, keeping, [IN_HBM])
    got_first, got_last, first, last = lax.optimization_barrier((got_first, got_last, first, last))
    late_first = passed(first, [(by, end) for _, by, _, end in late_ways])
    late_last = passed(last, [(by, end) for _, _, by, end in late_ways])

    both = [IN_HBM, ANYWHERE]

    def terms_of(first_half, last_half, positions):
        gram = cross(kept[:half], first_half) + cross(kept[half:], last_half)
        return summed(gram, positions)

    def slot_moved(first_half, last_half, terms):
        return rotation_of(
            selector(1),
            terms,
            [[kept, first_half], [kept, last_half]],
            [[0, 0], [half, 0]],
            half,
            both * 2,
        )

    _, prompt_keeping, first, last = slot_moved(got_first, got_last, terms_of(got_first, got_last, prompt))
    first, last, late_first, late_last = lax.optimization_barrier((first, last, late_first, late_last))
    token = passed(
        lax.slice(late_last, (0, 0), (16, 128)), [(half_cycle - 2, 0), (half_cycle - 1, 1)]
    )
    first, last, late_first, late_last, token = lax.optimization_barrier(
        (first, last, late_first, late_last, token)
    )
    from_first = passed(first, sends(prompt))
    beside = passed(last, [(source, by) for source, by, _ in ways])
    from_last = passed(last, sends(straight))
    from_far = passed(beside, [(by, end) for _, by, end in ways])

    terms = lax.cond(
        is_late,
        lambda: terms_of(late_first, late_last, late),
        lambda: (jnp.zeros((width, width), matrix.dtype),) * 2,
    )
    _, late_keeping, first, last = slot_moved(late_first, late_last, terms)
    from_late_first = passed(first, sends(late))
    from_late_last = passed(last, sends(late))

    keeping = jnp.where(is_late, late_keeping, prompt_keeping)
    got_first = jnp.where(is_late, late_first, got_first)
    got_last = jnp.where(is_late, late_last, got_last)
    out = rotated_rows([kept, got_first], [0, 0], half, keeping, both, matrix.shape)
    out = rotated_rows([kept, got_last], [half, 0], half, keeping, both, matrix.shape, out, half)
    out = place(1 - after_late, from_first, out, 0, [token])
    out = place((1 - after_late) * (1 - after_detoured), from_last, out, half)
    out = place(after_late, from_late_first, out, 0)
    out = place(after_late, from_late_last, out, half)
    return place(after_detoured, from_far, out, half)


def solution(mesh):
    placed = (P("samp", "pair"), P())
    return jax.shard_map(
        shards, mesh=mesh, in_specs=placed, out_specs=P("samp", "pair"), check_vma=False
    )
```

```python
import functools

import jax
import jax.numpy as jnp
from jax import lax
from jax.experimental import pallas as pl
from jax.experimental.pallas import tpu as pltpu
from jax.sharding import PartitionSpec as P

POLAR_STEPS = 5
TILE = 2048
VMEM_LIMIT = 48 * 1024 * 1024


coupling = 2.0
start_scale = 6.0

IN_VMEM = pl.BlockSpec(memory_space=pltpu.VMEM)
IN_SMEM = pl.BlockSpec(memory_space=pltpu.SMEM)
ANYWHERE = pl.BlockSpec(memory_space=pl.ANY)
IN_HBM = pl.BlockSpec(memory_space=pltpu.MemorySpace.HBM)


def reads_of(t, sources, starts, tile, block, arrivals):
    rows = pl.multiple_of(t * tile, tile)
    copies, at = [], 0
    for s, (source, start) in enumerate(zip(sources, starts)):
        span = source.shape[1]
        copies.append(
            pltpu.make_async_copy(
                source.at[pl.ds(pl.multiple_of(start + rows, tile), tile)],
                block.at[pl.ds(rows, tile), pl.ds(at, span)],
                arrivals.at[s, t],
            )
        )
        at += span
    return copies


def start_reads(sources, starts, tiles, tile, block, arrivals):
    def start(t, carry):
        for copy in reads_of(t, sources, starts, tile, block, arrivals):
            copy.start()
        return carry

    lax.fori_loop(0, tiles, start, 0)


def write_rotated(sources, starts, tiles, tile, block, arrivals, columns, rotated, out, first_row, departures):
    def write_of(t):
        rows = pl.multiple_of(t * tile, tile)
        return pltpu.make_async_copy(
            rotated.at[pl.ds(rows, tile)],
            out.at[pl.ds(pl.multiple_of(first_row + rows, tile), tile), pl.ds(0, rotated.shape[1])],
            departures.at[t],
        )

    def rotate(t, carry):
        for copy in reads_of(t, sources, starts, tile, block, arrivals):
            copy.wait()
        here = pl.ds(pl.multiple_of(t * tile, tile), tile)
        rotated[here, :] = jnp.dot(
            block[here, :], columns[...], preferred_element_type=jnp.float32
        ).astype(rotated.dtype)
        write_of(t).start()
        return carry

    def finish(t, carry):
        write_of(t).wait()
        return carry

    lax.fori_loop(0, tiles, rotate, 0)
    lax.fori_loop(0, tiles, finish, 0)


def polar_columns(selector, mine, other, moving, keeping, iterate):
    width = mine.shape[0]
    gram = mine[...].astype(jnp.float32) + other[...].astype(jnp.float32)
    frobenius = jnp.sqrt(jnp.sum(gram * gram, keepdims=True) + 1e-06)
    coupled = coupling * gram / frobenius
    row = lax.broadcasted_iota(jnp.int32, (width, width), 0)
    column = lax.broadcasted_iota(jnp.int32, (width, width), 1)
    diagonal = (row == column).astype(jnp.float32) / start_scale
    iterate[:width, :width] = diagonal
    iterate[width:, width:] = diagonal
    iterate[:width, width:] = -coupled / start_scale
    iterate[width:, :width] = coupled.T / start_scale

    def step(_, carry):
        current = iterate[...]
        rounded = current.astype(jnp.bfloat16)
        square = lax.dot_general(
            rounded, rounded, (((0,), (0,)), ((), ())), preferred_element_type=jnp.float32
        ).astype(jnp.bfloat16)
        iterate[...] = 1.5 * current - 0.5 * jnp.dot(
            rounded, square, preferred_element_type=jnp.float32
        )
        return carry

    lax.fori_loop(0, POLAR_STEPS, step, 0)
    first = iterate[:, :width].astype(jnp.bfloat16)
    second = iterate[:, width:].astype(jnp.bfloat16)
    second_stays = selector[0] == 1

    @pl.when(second_stays)
    def _():
        moving[...] = first
        keeping[...] = second

    @pl.when(jnp.logical_not(second_stays))
    def _():
        moving[...] = second
        keeping[...] = first


def rotation_kernel(tile, starts_of, *refs):
    selector, mine, other = refs[:3]
    counts = [len(starts) for starts in starts_of]
    parts = len(counts)
    tail = refs[3 + sum(counts) :]
    moving, keeping = tail[:2]
    outs, iterate, block, rotated = tail[2 : 2 + parts], tail[2 + parts], tail[3 + parts], tail[4 + parts]
    arrivals, departures = tail[5 + parts :]
    rows = outs[0].shape[0]
    tiles = rows // tile
    at, pieces = 3, []
    for k, count in enumerate(counts):
        here = pl.ds(k * rows, rows)
        pieces.append(
            (refs[at : at + count], starts_of[k], tiles, tile, block.at[here], arrivals.at[k])
        )
        at += count
    for piece in pieces:
        start_reads(*piece)
    polar_columns(selector, mine, other, moving, keeping, iterate)
    for k, (sources, starts, _, _, rows_of, arrived) in enumerate(pieces):
        write_rotated(
            sources, starts, tiles, tile, rows_of, arrived, moving,
            rotated.at[pl.ds(k * rows, rows)], outs[k], 0, departures.at[k],
        )


def rotation_of(selector, terms, parts, starts_of, rows, where):
    width = terms[0].shape[0]
    tile = min(TILE, rows)
    counts = [len(part) for part in parts]
    columns = jax.ShapeDtypeStruct((2 * width, width), jnp.bfloat16)
    moved = jax.ShapeDtypeStruct((rows, width), jnp.bfloat16)
    return pl.pallas_call(
        functools.partial(rotation_kernel, tile, starts_of),
        out_shape=[columns, columns] + [moved] * len(parts),
        in_specs=[IN_SMEM, IN_VMEM, IN_VMEM] + where,
        out_specs=[IN_VMEM, IN_VMEM] + [IN_HBM] * len(parts),
        scratch_shapes=[
            pltpu.VMEM((2 * width, 2 * width), jnp.float32),
            pltpu.VMEM((len(parts) * rows, 2 * width), jnp.bfloat16),
            pltpu.VMEM((len(parts) * rows, width), jnp.bfloat16),
            pltpu.SemaphoreType.DMA((len(parts), max(counts), rows // tile)),
            pltpu.SemaphoreType.DMA((len(parts), rows // tile)),
        ],
        compiler_params=pltpu.CompilerParams(vmem_limit_bytes=VMEM_LIMIT),
        cost_estimate=pl.CostEstimate(
            flops=2 * 2 * POLAR_STEPS * (2 * width) ** 3 + 4 * len(parts) * rows * width**2,
            bytes_accessed=10 * width**2 + 6 * len(parts) * rows * width,
            transcendentals=0,
        ),
    )(selector, *terms, *[source for part in parts for source in part])


def rotated_kernel(starts, tile, rows, first_row, *refs):
    columns, sources = refs[0], refs[1 : 1 + len(starts)]
    out, block, rotated, arrivals, departures = refs[-5:]
    tiles = rows // tile
    start_reads(sources, starts, tiles, tile, block, arrivals)
    write_rotated(
        sources, starts, tiles, tile, block, arrivals, columns, rotated, out, first_row, departures
    )


def rotated_rows(sources, starts, rows, columns, where, shape=None, out=None, first_row=0):
    width = columns.shape[1]
    tile = min(TILE, rows)
    before = [] if out is None else [out]
    return pl.pallas_call(
        functools.partial(rotated_kernel, starts, tile, rows, first_row),
        out_shape=jax.ShapeDtypeStruct(shape or (rows, width), columns.dtype),
        in_specs=[IN_VMEM] + where + [IN_HBM] * len(before),
        out_specs=IN_HBM,
        input_output_aliases={1 + len(sources): 0} if before else {},
        scratch_shapes=[
            pltpu.VMEM((rows, 2 * width), jnp.bfloat16),
            pltpu.VMEM((rows, width), jnp.bfloat16),
            pltpu.SemaphoreType.DMA((len(sources), rows // tile)),
            pltpu.SemaphoreType.DMA((rows // tile,)),
        ],
        compiler_params=pltpu.CompilerParams(vmem_limit_bytes=VMEM_LIMIT),
        cost_estimate=pl.CostEstimate(
            flops=4 * rows * width**2, bytes_accessed=6 * rows * width, transcendentals=0
        ),
    )(columns, *sources, *before)


def place_kernel(tile, first_row, wanted, source, _, *refs):
    out, block, arrivals, departures = refs[-4:]
    rows, width = source.shape

    @pl.when(wanted[0] == 1)
    def _():
        reads = [
            pltpu.make_async_copy(
                source.at[pl.ds(t * tile, tile)], block.at[pl.ds(t * tile, tile)], arrivals.at[t]
            )
            for t in range(rows // tile)
        ]
        writes = [
            pltpu.make_async_copy(
                block.at[pl.ds(t * tile, tile)],
                out.at[pl.ds(first_row + t * tile, tile), pl.ds(width, width)],
                departures.at[t],
            )
            for t in range(rows // tile)
        ]
        for read in reads:
            read.start()
        for read, write in zip(reads, writes):
            read.wait()
            write.start()
        for write in writes:
            write.wait()


def place(wanted, source, out, first_row, after=()):
    rows, width = source.shape
    tile = min(TILE, rows)
    return pl.pallas_call(
        functools.partial(place_kernel, tile, first_row),
        out_shape=jax.ShapeDtypeStruct(out.shape, out.dtype),
        in_specs=[IN_SMEM, ANYWHERE, IN_HBM] + [ANYWHERE] * len(after),
        out_specs=IN_HBM,
        input_output_aliases={2: 0},
        scratch_shapes=[
            pltpu.VMEM((rows, width), jnp.bfloat16),
            pltpu.SemaphoreType.DMA((rows // tile,)),
            pltpu.SemaphoreType.DMA((rows // tile,)),
        ],
        compiler_params=pltpu.CompilerParams(vmem_limit_bytes=VMEM_LIMIT),
        cost_estimate=pl.CostEstimate(flops=0, bytes_accessed=4 * rows * width, transcendentals=0),
    )(wanted, source, out, *after)


def summed(value, positions):
    length, cycle_size = lax.axis_size("samp"), lax.axis_size("pair")
    total = value.astype(jnp.bfloat16)
    if length & (length - 1):
        return lax.psum(total, "samp"), jnp.zeros_like(total)
    other = jnp.zeros_like(total)
    step = 1
    while step < length:
        if step > 1:
            total = (total.astype(jnp.float32) + other.astype(jnp.float32)).astype(jnp.bfloat16)
        pairs = [(i * cycle_size + p, (i ^ step) * cycle_size + p) for i in range(length) for p in positions]
        other = lax.ppermute(total, ("samp", "pair"), pairs)
        step *= 2
    return total, other


def cross(first, second):
    return lax.dot_general(
        first, second, (((0,), (0,)), ((), ())), preferred_element_type=jnp.float32
    )


def shards(matrix, tournament):
    cycle_size = lax.axis_size("pair")
    half_cycle = cycle_size // 2
    position = lax.axis_index("pair")
    rows, width = matrix.shape[0], matrix.shape[1] // 2
    half = rows // 2

    def target(p):
        return (p + half_cycle + 1) % cycle_size

    def among(positions):
        found = sum((position == p).astype(jnp.int32) for p in positions)
        return found.reshape((1,))

    def passed(value, pairs):
        return lax.ppermute(value, "pair", pairs)

    def selector(tourney):
        slot_index = (position + half_cycle * (tourney % 2)) % cycle_size
        return lax.dynamic_slice(tournament[tourney], (slot_index,), (1,))

    def sends(positions):
        return [(p, target(p)) for p in positions]

    whole = list(range(cycle_size))
    late = [half_cycle - 1, cycle_size - 1]
    to_late = [p for p in whole if target(p) in late]
    others = [p for p in whole if p not in to_late]
    prompt = [p for p in whole if p not in late]
    late_ways = [
        (cycle_size - 2, half_cycle, cycle_size - 1, half_cycle - 1),
        (half_cycle - 2, half_cycle - 2, half_cycle - 1, cycle_size - 1),
    ]
    ways = [(0, half_cycle - 1, target(0)), (cycle_size - 2, half_cycle + 1, half_cycle - 1)]
    detoured = [source for source, _, _ in ways]
    straight = [p for p in prompt if p not in detoured]
    is_late = among(late)[0] == 1
    after_late = among([target(p) for p in late])
    after_detoured = among([target(p) for p in detoured])

    gram = cross(matrix[:, :width], matrix[:, width:])
    _, keeping, first, last = rotation_of(
        selector(0), summed(gram, whole), [[matrix], [matrix]], [[0], [half]], half, [IN_HBM] * 2
    )
    got_first = passed(first, sends(others) + [(source, by) for source, _, by, _ in late_ways])
    got_last = passed(last, sends(others))
    relayed = passed(last, [(source, by) for source, by, _, _ in late_ways])
    kept = rotated_rows([matrix], [0], rows, keeping, [IN_HBM])
    got_first, got_last, relayed = lax.optimization_barrier((got_first, got_last, relayed))
    late_first = passed(got_first, [(by, end) for _, _, by, end in late_ways])
    late_last = passed(relayed, [(by, end) for _, by, _, end in late_ways])

    both = [IN_HBM, ANYWHERE]

    def terms_of(first_half, last_half, positions):
        gram = cross(kept[:half], first_half) + cross(kept[half:], last_half)
        return summed(gram, positions)

    def slot_moved(first_half, last_half, terms):
        return rotation_of(
            selector(1),
            terms,
            [[kept, first_half], [kept, last_half]],
            [[0, 0], [half, 0]],
            half,
            both * 2,
        )

    _, prompt_keeping, first, last = slot_moved(got_first, got_last, terms_of(got_first, got_last, prompt))
    first, last, late_first, late_last, token = lax.optimization_barrier(
        (first, last, late_first, late_last, jnp.zeros((16, 128), matrix.dtype))
    )
    token = passed(token, [(half_cycle - 2, 0), (cycle_size - 1, cycle_size - 2)])
    first, last, late_first, late_last, token = lax.optimization_barrier(
        (first, last, late_first, late_last, token)
    )
    from_first = passed(first, sends(prompt))
    from_last = passed(last, sends(straight) + [(source, by) for source, by, _ in ways])
    from_far = passed(from_last, [(by, end) for _, by, end in ways])

    terms = lax.cond(
        is_late,
        lambda: terms_of(late_first, late_last, late),
        lambda: (jnp.zeros((width, width), matrix.dtype),) * 2,
    )
    _, late_keeping, first, last = slot_moved(late_first, late_last, terms)
    from_late_first = passed(first, sends(late))
    from_late_last = passed(last, sends(late))

    keeping = jnp.where(is_late, late_keeping, prompt_keeping)
    got_first = jnp.where(is_late, late_first, got_first)
    got_last = jnp.where(is_late, late_last, got_last)
    out = rotated_rows([kept, got_first], [0, 0], half, keeping, both, matrix.shape)
    out = rotated_rows([kept, got_last], [half, 0], half, keeping, both, matrix.shape, out, half)
    out = place((1 - after_late) * (1 - after_detoured), from_last, out, half, [token])
    out = place(1 - after_late, from_first, out, 0)
    out = place(after_late, from_late_first, out, 0)
    out = place(after_late, from_late_last, out, half)
    return place(after_detoured, from_far, out, half)


def solution(mesh):
    placed = (P("samp", "pair"), P())
    return jax.shard_map(
        shards, mesh=mesh, in_specs=placed, out_specs=P("samp", "pair"), check_vma=False
    )
```

```python
import functools

import jax
import jax.numpy as jnp
from jax import lax
from jax.experimental import pallas as pl
from jax.experimental.pallas import tpu as pltpu
from jax.sharding import PartitionSpec as P

POLAR_STEPS = 5
TILE = 2048
VMEM_LIMIT = 48 * 1024 * 1024


coupling = 2.0
start_scale = 6.0

IN_VMEM = pl.BlockSpec(memory_space=pltpu.VMEM)
IN_SMEM = pl.BlockSpec(memory_space=pltpu.SMEM)
ANYWHERE = pl.BlockSpec(memory_space=pl.ANY)
IN_HBM = pl.BlockSpec(memory_space=pltpu.MemorySpace.HBM)


def reads_of(t, sources, starts, tile, block, arrivals):
    rows = pl.multiple_of(t * tile, tile)
    copies, at = [], 0
    for s, (source, start) in enumerate(zip(sources, starts)):
        span = source.shape[1]
        copies.append(
            pltpu.make_async_copy(
                source.at[pl.ds(pl.multiple_of(start + rows, tile), tile)],
                block.at[pl.ds(rows, tile), pl.ds(at, span)],
                arrivals.at[s, t],
            )
        )
        at += span
    return copies


def start_reads(sources, starts, tiles, tile, block, arrivals):
    def start(t, carry):
        for copy in reads_of(t, sources, starts, tile, block, arrivals):
            copy.start()
        return carry

    lax.fori_loop(0, tiles, start, 0)


def write_rotated(sources, starts, tiles, tile, block, arrivals, columns, rotated, out, first_row, departures):
    def write_of(t):
        rows = pl.multiple_of(t * tile, tile)
        return pltpu.make_async_copy(
            rotated.at[pl.ds(rows, tile)],
            out.at[pl.ds(pl.multiple_of(first_row + rows, tile), tile), pl.ds(0, rotated.shape[1])],
            departures.at[t],
        )

    def rotate(t, carry):
        for copy in reads_of(t, sources, starts, tile, block, arrivals):
            copy.wait()
        here = pl.ds(pl.multiple_of(t * tile, tile), tile)
        rotated[here, :] = jnp.dot(
            block[here, :], columns[...], preferred_element_type=jnp.float32
        ).astype(rotated.dtype)
        write_of(t).start()
        return carry

    def finish(t, carry):
        write_of(t).wait()
        return carry

    lax.fori_loop(0, tiles, rotate, 0)
    lax.fori_loop(0, tiles, finish, 0)


def polar_columns(selector, mine, other, moving, keeping, iterate):
    width = mine.shape[0]
    gram = mine[...].astype(jnp.float32) + other[...].astype(jnp.float32)
    frobenius = jnp.sqrt(jnp.sum(gram * gram, keepdims=True) + 1e-06)
    coupled = coupling * gram / frobenius
    row = lax.broadcasted_iota(jnp.int32, (width, width), 0)
    column = lax.broadcasted_iota(jnp.int32, (width, width), 1)
    diagonal = (row == column).astype(jnp.float32) / start_scale
    iterate[:width, :width] = diagonal
    iterate[width:, width:] = diagonal
    iterate[:width, width:] = -coupled / start_scale
    iterate[width:, :width] = coupled.T / start_scale

    def step(_, carry):
        current = iterate[...]
        rounded = current.astype(jnp.bfloat16)
        square = lax.dot_general(
            rounded, rounded, (((0,), (0,)), ((), ())), preferred_element_type=jnp.float32
        ).astype(jnp.bfloat16)
        iterate[...] = 1.5 * current - 0.5 * jnp.dot(
            rounded, square, preferred_element_type=jnp.float32
        )
        return carry

    lax.fori_loop(0, POLAR_STEPS, step, 0, unroll=True)
    first = iterate[:, :width].astype(jnp.bfloat16)
    second = iterate[:, width:].astype(jnp.bfloat16)
    second_stays = selector[0] == 1

    @pl.when(second_stays)
    def _():
        moving[...] = first
        keeping[...] = second

    @pl.when(jnp.logical_not(second_stays))
    def _():
        moving[...] = second
        keeping[...] = first


def rotation_kernel(tile, starts_of, *refs):
    selector, mine, other = refs[:3]
    counts = [len(starts) for starts in starts_of]
    parts = len(counts)
    tail = refs[3 + sum(counts) :]
    moving, keeping = tail[:2]
    outs, iterate, block, rotated = tail[2 : 2 + parts], tail[2 + parts], tail[3 + parts], tail[4 + parts]
    arrivals, departures = tail[5 + parts :]
    rows = outs[0].shape[0]
    tiles = rows // tile
    at, pieces = 3, []
    for k, count in enumerate(counts):
        here = pl.ds(k * rows, rows)
        pieces.append(
            (refs[at : at + count], starts_of[k], tiles, tile, block.at[here], arrivals.at[k])
        )
        at += count
    for piece in pieces:
        start_reads(*piece)
    polar_columns(selector, mine, other, moving, keeping, iterate)
    for k, (sources, starts, _, _, rows_of, arrived) in enumerate(pieces):
        write_rotated(
            sources, starts, tiles, tile, rows_of, arrived, moving,
            rotated.at[pl.ds(k * rows, rows)], outs[k], 0, departures.at[k],
        )


def rotation_of(selector, terms, parts, starts_of, rows, where):
    width = terms[0].shape[0]
    tile = min(TILE, rows)
    counts = [len(part) for part in parts]
    columns = jax.ShapeDtypeStruct((2 * width, width), jnp.bfloat16)
    moved = jax.ShapeDtypeStruct((rows, width), jnp.bfloat16)
    return pl.pallas_call(
        functools.partial(rotation_kernel, tile, starts_of),
        out_shape=[columns, columns] + [moved] * len(parts),
        in_specs=[IN_SMEM, IN_VMEM, IN_VMEM] + where,
        out_specs=[IN_VMEM, IN_VMEM] + [IN_HBM] * len(parts),
        scratch_shapes=[
            pltpu.VMEM((2 * width, 2 * width), jnp.float32),
            pltpu.VMEM((len(parts) * rows, 2 * width), jnp.bfloat16),
            pltpu.VMEM((len(parts) * rows, width), jnp.bfloat16),
            pltpu.SemaphoreType.DMA((len(parts), max(counts), rows // tile)),
            pltpu.SemaphoreType.DMA((len(parts), rows // tile)),
        ],
        compiler_params=pltpu.CompilerParams(vmem_limit_bytes=VMEM_LIMIT),
        cost_estimate=pl.CostEstimate(
            flops=2 * 2 * POLAR_STEPS * (2 * width) ** 3 + 4 * len(parts) * rows * width**2,
            bytes_accessed=10 * width**2 + 6 * len(parts) * rows * width,
            transcendentals=0,
        ),
    )(selector, *terms, *[source for part in parts for source in part])


def rotated_kernel(starts, tile, rows, first_row, *refs):
    columns, sources = refs[0], refs[1 : 1 + len(starts)]
    out, block, rotated, arrivals, departures = refs[-5:]
    tiles = rows // tile
    start_reads(sources, starts, tiles, tile, block, arrivals)
    write_rotated(
        sources, starts, tiles, tile, block, arrivals, columns, rotated, out, first_row, departures
    )


def rotated_rows(sources, starts, rows, columns, where, shape=None, out=None, first_row=0):
    width = columns.shape[1]
    tile = min(TILE, rows)
    before = [] if out is None else [out]
    return pl.pallas_call(
        functools.partial(rotated_kernel, starts, tile, rows, first_row),
        out_shape=jax.ShapeDtypeStruct(shape or (rows, width), columns.dtype),
        in_specs=[IN_VMEM] + where + [IN_HBM] * len(before),
        out_specs=IN_HBM,
        input_output_aliases={1 + len(sources): 0} if before else {},
        scratch_shapes=[
            pltpu.VMEM((rows, 2 * width), jnp.bfloat16),
            pltpu.VMEM((rows, width), jnp.bfloat16),
            pltpu.SemaphoreType.DMA((len(sources), rows // tile)),
            pltpu.SemaphoreType.DMA((rows // tile,)),
        ],
        compiler_params=pltpu.CompilerParams(vmem_limit_bytes=VMEM_LIMIT),
        cost_estimate=pl.CostEstimate(
            flops=4 * rows * width**2, bytes_accessed=6 * rows * width, transcendentals=0
        ),
    )(columns, *sources, *before)


def place_kernel(tile, first_row, wanted, source, _, *refs):
    out, block, arrivals, departures = refs[-4:]
    rows, width = source.shape

    @pl.when(wanted[0] == 1)
    def _():
        reads = [
            pltpu.make_async_copy(
                source.at[pl.ds(t * tile, tile)], block.at[pl.ds(t * tile, tile)], arrivals.at[t]
            )
            for t in range(rows // tile)
        ]
        writes = [
            pltpu.make_async_copy(
                block.at[pl.ds(t * tile, tile)],
                out.at[pl.ds(first_row + t * tile, tile), pl.ds(width, width)],
                departures.at[t],
            )
            for t in range(rows // tile)
        ]
        for read in reads:
            read.start()
        for read, write in zip(reads, writes):
            read.wait()
            write.start()
        for write in writes:
            write.wait()


def place(wanted, source, out, first_row, after=()):
    rows, width = source.shape
    tile = min(TILE, rows)
    return pl.pallas_call(
        functools.partial(place_kernel, tile, first_row),
        out_shape=jax.ShapeDtypeStruct(out.shape, out.dtype),
        in_specs=[IN_SMEM, ANYWHERE, IN_HBM] + [ANYWHERE] * len(after),
        out_specs=IN_HBM,
        input_output_aliases={2: 0},
        scratch_shapes=[
            pltpu.VMEM((rows, width), jnp.bfloat16),
            pltpu.SemaphoreType.DMA((rows // tile,)),
            pltpu.SemaphoreType.DMA((rows // tile,)),
        ],
        compiler_params=pltpu.CompilerParams(vmem_limit_bytes=VMEM_LIMIT),
        cost_estimate=pl.CostEstimate(flops=0, bytes_accessed=4 * rows * width, transcendentals=0),
    )(wanted, source, out, *after)


def summed(value, positions):
    length, cycle_size = lax.axis_size("samp"), lax.axis_size("pair")
    total = value.astype(jnp.bfloat16)
    if length & (length - 1):
        return lax.psum(total, "samp"), jnp.zeros_like(total)
    other = jnp.zeros_like(total)
    step = 1
    while step < length:
        if step > 1:
            total = (total.astype(jnp.float32) + other.astype(jnp.float32)).astype(jnp.bfloat16)
        pairs = [(i * cycle_size + p, (i ^ step) * cycle_size + p) for i in range(length) for p in positions]
        other = lax.ppermute(total, ("samp", "pair"), pairs)
        step *= 2
    return total, other


def whole_gram_kernel(tile, matrix, gram, block, total, arrivals):
    rows, width = matrix.shape[0], matrix.shape[1] // 2

    def read_of(t):
        here = pl.ds(pl.multiple_of(t * tile, tile), tile)
        return pltpu.make_async_copy(matrix.at[here], block.at[here], arrivals.at[t])

    def start(t, carry):
        read_of(t).start()
        return carry

    def add(t, carry):
        read_of(t).wait()
        here = pl.ds(pl.multiple_of(t * tile, tile), tile)
        total[...] += cross(block[here, :width], block[here, width:])
        return carry

    lax.fori_loop(0, rows // tile, start, 0)
    total[...] = jnp.zeros_like(total)
    lax.fori_loop(0, rows // tile, add, 0)
    gram[...] = total[...].astype(gram.dtype)


def whole_gram(matrix):
    rows, width = matrix.shape[0], matrix.shape[1] // 2
    tile = min(1024, rows)
    return pl.pallas_call(
        functools.partial(whole_gram_kernel, tile),
        out_shape=jax.ShapeDtypeStruct((width, width), matrix.dtype),
        in_specs=[IN_HBM],
        out_specs=IN_VMEM,
        scratch_shapes=[
            pltpu.VMEM(matrix.shape, matrix.dtype),
            pltpu.VMEM((width, width), jnp.float32),
            pltpu.SemaphoreType.DMA((rows // tile,)),
        ],
        compiler_params=pltpu.CompilerParams(vmem_limit_bytes=VMEM_LIMIT),
        cost_estimate=pl.CostEstimate(
            flops=2 * rows * width**2, bytes_accessed=4 * rows * width, transcendentals=0
        ),
    )(matrix)


def cross(first, second):
    return lax.dot_general(
        first, second, (((0,), (0,)), ((), ())), preferred_element_type=jnp.float32
    )


def shards(matrix, tournament):
    cycle_size = lax.axis_size("pair")
    half_cycle = cycle_size // 2
    position = lax.axis_index("pair")
    rows, width = matrix.shape[0], matrix.shape[1] // 2
    half = rows // 2

    def target(p):
        return (p + half_cycle + 1) % cycle_size

    def among(positions):
        found = sum((position == p).astype(jnp.int32) for p in positions)
        return found.reshape((1,))

    def passed(value, pairs):
        return lax.ppermute(value, "pair", pairs)

    def selector(tourney):
        slot_index = (position + half_cycle * (tourney % 2)) % cycle_size
        return lax.dynamic_slice(tournament[tourney], (slot_index,), (1,))

    def sends(positions):
        return [(p, target(p)) for p in positions]

    whole = list(range(cycle_size))
    late = [half_cycle - 1, cycle_size - 1]
    to_late = [p for p in whole if target(p) in late]
    others = [p for p in whole if p not in to_late]
    prompt = [p for p in whole if p not in late]
    late_ways = [
        (cycle_size - 2, half_cycle, cycle_size - 1, half_cycle - 1),
        (half_cycle - 2, half_cycle - 2, half_cycle - 1, cycle_size - 1),
    ]
    ways = [(0, half_cycle - 1, target(0)), (cycle_size - 2, half_cycle + 1, half_cycle - 1)]
    detoured = [source for source, _, _ in ways]
    straight = [p for p in prompt if p not in detoured]
    is_late = among(late)[0] == 1
    after_late = among([target(p) for p in late])
    after_detoured = among([target(p) for p in detoured])

    gram = whole_gram(matrix)
    _, keeping, first, last = rotation_of(
        selector(0), summed(gram, whole), [[matrix], [matrix]], [[0], [half]], half, [IN_HBM] * 2
    )
    got_first = passed(first, sends(others) + [(source, by) for source, _, by, _ in late_ways])
    got_last = passed(last, sends(others))
    relayed = passed(last, [(source, by) for source, by, _, _ in late_ways])
    kept = rotated_rows([matrix], [0], rows, keeping, [IN_HBM])
    got_first, got_last, relayed = lax.optimization_barrier((got_first, got_last, relayed))
    late_first = passed(got_first, [(by, end) for _, _, by, end in late_ways])
    late_last = passed(relayed, [(by, end) for _, by, _, end in late_ways])

    both = [IN_HBM, ANYWHERE]

    def terms_of(first_half, last_half, positions):
        gram = cross(kept[:half], first_half) + cross(kept[half:], last_half)
        return summed(gram, positions)

    def slot_moved(first_half, last_half, terms):
        return rotation_of(
            selector(1),
            terms,
            [[kept, first_half], [kept, last_half]],
            [[0, 0], [half, 0]],
            half,
            both * 2,
        )

    _, prompt_keeping, first, last = slot_moved(got_first, got_last, terms_of(got_first, got_last, prompt))
    first, last, late_first, late_last, token = lax.optimization_barrier(
        (first, last, late_first, late_last, jnp.zeros((16, 128), matrix.dtype))
    )
    token = passed(token, [(half_cycle - 2, cycle_size - 2)])
    first, last, late_first, late_last, token = lax.optimization_barrier(
        (first, last, late_first, late_last, token)
    )
    from_first = passed(first, sends(prompt))
    from_last = passed(last, sends(straight) + [(source, by) for source, by, _ in ways])
    from_far = passed(from_last, [(by, end) for _, by, end in ways])

    terms = lax.cond(
        is_late,
        lambda: terms_of(late_first, late_last, late),
        lambda: (jnp.zeros((width, width), matrix.dtype),) * 2,
    )
    _, late_keeping, first, last = slot_moved(late_first, late_last, terms)
    from_late_first = passed(first, sends(late))
    from_late_last = passed(last, sends(late))

    keeping = jnp.where(is_late, late_keeping, prompt_keeping)
    got_first = jnp.where(is_late, late_first, got_first)
    got_last = jnp.where(is_late, late_last, got_last)
    out = rotated_rows([kept, got_first], [0, 0], half, keeping, both, matrix.shape)
    out = rotated_rows([kept, got_last], [half, 0], half, keeping, both, matrix.shape, out, half)
    out = place((1 - after_late) * (1 - after_detoured), from_last, out, half, [token])
    out = place(1 - after_late, from_first, out, 0)
    out = place(after_late, from_late_first, out, 0)
    out = place(after_late, from_late_last, out, half)
    return place(after_detoured, from_far, out, half)


def solution(mesh):
    placed = (P("samp", "pair"), P())
    return jax.shard_map(
        shards, mesh=mesh, in_specs=placed, out_specs=P("samp", "pair"), check_vma=False
    )
```

```python
import functools

import jax
import jax.numpy as jnp
from jax import lax
from jax.experimental import pallas as pl
from jax.experimental.pallas import tpu as pltpu
from jax.sharding import PartitionSpec as P

POLAR_STEPS = 5
TILE = 2048
VMEM_LIMIT = 48 * 1024 * 1024


coupling = 2.0
start_scale = 6.0

IN_VMEM = pl.BlockSpec(memory_space=pltpu.VMEM)
IN_SMEM = pl.BlockSpec(memory_space=pltpu.SMEM)
ANYWHERE = pl.BlockSpec(memory_space=pl.ANY)
IN_HBM = pl.BlockSpec(memory_space=pltpu.MemorySpace.HBM)


def reads_of(t, sources, starts, tile, block, arrivals):
    rows = pl.multiple_of(t * tile, tile)
    copies, at = [], 0
    for s, (source, start) in enumerate(zip(sources, starts)):
        span = source.shape[1]
        copies.append(
            pltpu.make_async_copy(
                source.at[pl.ds(pl.multiple_of(start + rows, tile), tile)],
                block.at[pl.ds(rows, tile), pl.ds(at, span)],
                arrivals.at[s, t],
            )
        )
        at += span
    return copies


def start_reads(sources, starts, tiles, tile, block, arrivals):
    def start(t, carry):
        for copy in reads_of(t, sources, starts, tile, block, arrivals):
            copy.start()
        return carry

    lax.fori_loop(0, tiles, start, 0)


def write_rotated(sources, starts, tiles, tile, block, arrivals, columns, rotated, out, first_row, departures):
    def write_of(t):
        rows = pl.multiple_of(t * tile, tile)
        return pltpu.make_async_copy(
            rotated.at[pl.ds(rows, tile)],
            out.at[pl.ds(pl.multiple_of(first_row + rows, tile), tile), pl.ds(0, rotated.shape[1])],
            departures.at[t],
        )

    def rotate(t, carry):
        for copy in reads_of(t, sources, starts, tile, block, arrivals):
            copy.wait()
        here = pl.ds(pl.multiple_of(t * tile, tile), tile)
        rotated[here, :] = lax.dot_general(
            block[here, :], columns[...], (((1,), (1,)), ((), ())), preferred_element_type=jnp.float32
        ).astype(rotated.dtype)
        write_of(t).start()
        return carry

    def wait(t, carry):
        write_of(t).wait()
        return carry

    lax.fori_loop(0, tiles, rotate, 0)
    return lambda: lax.fori_loop(0, tiles, wait, 0)


def polar_columns(selector, mine, other, moving, keeping, iterate):
    width = mine.shape[0]
    gram = mine[...].astype(jnp.float32) + other[...].astype(jnp.float32)
    frobenius = jnp.sqrt(jnp.sum(gram * gram, keepdims=True) + 1e-06)
    coupled = coupling * gram / frobenius
    row = lax.broadcasted_iota(jnp.int32, (width, width), 0)
    column = lax.broadcasted_iota(jnp.int32, (width, width), 1)
    diagonal = (row == column).astype(jnp.float32) / start_scale
    iterate[:width, :width] = diagonal
    iterate[width:, width:] = diagonal
    iterate[:width, width:] = coupled / start_scale
    iterate[width:, :width] = -coupled.T / start_scale

    def step(_, carry):
        current = iterate[...]
        rounded = current.astype(jnp.bfloat16)
        square = lax.dot_general(
            rounded, rounded, (((1,), (1,)), ((), ())), preferred_element_type=jnp.float32
        ).astype(jnp.bfloat16)
        iterate[...] = 1.5 * current - 0.5 * jnp.dot(
            square, rounded, preferred_element_type=jnp.float32
        )
        return carry

    lax.fori_loop(0, POLAR_STEPS, step, 0, unroll=True)
    first = iterate[:width, :].astype(jnp.bfloat16)
    second = iterate[width:, :].astype(jnp.bfloat16)
    second_stays = selector[0] == 1

    @pl.when(second_stays)
    def _():
        moving[...] = first
        keeping[...] = second

    @pl.when(jnp.logical_not(second_stays))
    def _():
        moving[...] = second
        keeping[...] = first


def rotation_kernel(tile, starts_of, *refs):
    selector, mine, other = refs[:3]
    counts = [len(starts) for starts in starts_of]
    parts = len(counts)
    tail = refs[3 + sum(counts) :]
    kept_columns, outs = tail[0], tail[1 : 1 + parts]
    iterate, moving, keeping, block, rotated, arrivals, departures, departure = tail[1 + parts :]
    rows = outs[0].shape[0]
    tiles = rows // tile
    at, pieces = 3, []
    for k, count in enumerate(counts):
        here = pl.ds(k * rows, rows)
        pieces.append(
            (refs[at : at + count], starts_of[k], tiles, tile, block.at[here], arrivals.at[k])
        )
        at += count
    for piece in pieces:
        start_reads(*piece)
    polar_columns(selector, mine, other, moving, keeping, iterate)
    waits = [
        write_rotated(
            *piece, moving, rotated.at[pl.ds(k * rows, rows)], outs[k], 0, departures.at[k]
        )
        for k, piece in enumerate(pieces)
    ]
    write = pltpu.make_async_copy(keeping, kept_columns, departure)
    write.start()
    for wait in waits:
        wait()
    write.wait()


def rotation_of(selector, terms, parts, starts_of, rows, where):
    width = terms[0].shape[0]
    tile = min(TILE, rows)
    counts = [len(part) for part in parts]
    columns = (width, 2 * width)
    moved = jax.ShapeDtypeStruct((rows, width), jnp.bfloat16)
    return pl.pallas_call(
        functools.partial(rotation_kernel, tile, starts_of),
        out_shape=[jax.ShapeDtypeStruct(columns, jnp.bfloat16)] + [moved] * len(parts),
        in_specs=[IN_SMEM, IN_VMEM, IN_VMEM] + where,
        out_specs=[IN_HBM] * (1 + len(parts)),
        scratch_shapes=[
            pltpu.VMEM((2 * width, 2 * width), jnp.float32),
            pltpu.VMEM(columns, jnp.bfloat16),
            pltpu.VMEM(columns, jnp.bfloat16),
            pltpu.VMEM((len(parts) * rows, 2 * width), jnp.bfloat16),
            pltpu.VMEM((len(parts) * rows, width), jnp.bfloat16),
            pltpu.SemaphoreType.DMA((len(parts), max(counts), rows // tile)),
            pltpu.SemaphoreType.DMA((len(parts), rows // tile)),
            pltpu.SemaphoreType.DMA(()),
        ],
        compiler_params=pltpu.CompilerParams(vmem_limit_bytes=VMEM_LIMIT),
        cost_estimate=pl.CostEstimate(
            flops=2 * 2 * POLAR_STEPS * (2 * width) ** 3 + 4 * len(parts) * rows * width**2,
            bytes_accessed=10 * width**2 + 6 * len(parts) * rows * width,
            transcendentals=0,
        ),
    )(selector, *terms, *[source for part in parts for source in part])


def rotated_kernel(starts, tile, rows, first_row, *refs):
    columns, sources = refs[0], refs[1 : 1 + len(starts)]
    out, block, rotated, arrivals, departures = refs[-5:]
    tiles = rows // tile
    start_reads(sources, starts, tiles, tile, block, arrivals)
    write_rotated(
        sources, starts, tiles, tile, block, arrivals, columns, rotated, out, first_row, departures
    )()


def rotated_rows(sources, starts, rows, columns, where, shape=None, out=None, first_row=0):
    width = columns.shape[0]
    tile = min(TILE, rows)
    before = [] if out is None else [out]
    return pl.pallas_call(
        functools.partial(rotated_kernel, starts, tile, rows, first_row),
        out_shape=jax.ShapeDtypeStruct(shape or (rows, width), columns.dtype),
        in_specs=[IN_VMEM] + where + [IN_HBM] * len(before),
        out_specs=IN_HBM,
        input_output_aliases={1 + len(sources): 0} if before else {},
        scratch_shapes=[
            pltpu.VMEM((rows, 2 * width), jnp.bfloat16),
            pltpu.VMEM((rows, width), jnp.bfloat16),
            pltpu.SemaphoreType.DMA((len(sources), rows // tile)),
            pltpu.SemaphoreType.DMA((rows // tile,)),
        ],
        compiler_params=pltpu.CompilerParams(vmem_limit_bytes=VMEM_LIMIT),
        cost_estimate=pl.CostEstimate(
            flops=4 * rows * width**2, bytes_accessed=6 * rows * width, transcendentals=0
        ),
    )(columns, *sources, *before)


def place_kernel(tile, first_row, wanted, source, _, *refs):
    out, block, arrivals, departures = refs[-4:]
    rows, width = source.shape

    @pl.when(wanted[0] == 1)
    def _():
        reads = [
            pltpu.make_async_copy(
                source.at[pl.ds(t * tile, tile)], block.at[pl.ds(t * tile, tile)], arrivals.at[t]
            )
            for t in range(rows // tile)
        ]
        writes = [
            pltpu.make_async_copy(
                block.at[pl.ds(t * tile, tile)],
                out.at[pl.ds(first_row + t * tile, tile), pl.ds(width, width)],
                departures.at[t],
            )
            for t in range(rows // tile)
        ]
        for read in reads:
            read.start()
        for read, write in zip(reads, writes):
            read.wait()
            write.start()
        for write in writes:
            write.wait()


def place(wanted, source, out, first_row, after=()):
    rows, width = source.shape
    tile = min(TILE, rows)
    return pl.pallas_call(
        functools.partial(place_kernel, tile, first_row),
        out_shape=jax.ShapeDtypeStruct(out.shape, out.dtype),
        in_specs=[IN_SMEM, ANYWHERE, IN_HBM] + [ANYWHERE] * len(after),
        out_specs=IN_HBM,
        input_output_aliases={2: 0},
        scratch_shapes=[
            pltpu.VMEM((rows, width), jnp.bfloat16),
            pltpu.SemaphoreType.DMA((rows // tile,)),
            pltpu.SemaphoreType.DMA((rows // tile,)),
        ],
        compiler_params=pltpu.CompilerParams(vmem_limit_bytes=VMEM_LIMIT),
        cost_estimate=pl.CostEstimate(flops=0, bytes_accessed=4 * rows * width, transcendentals=0),
    )(wanted, source, out, *after)


def summed(value, positions):
    length, cycle_size = lax.axis_size("samp"), lax.axis_size("pair")
    total = value.astype(jnp.bfloat16)
    if length & (length - 1):
        return lax.psum(total, "samp"), jnp.zeros_like(total)
    other = jnp.zeros_like(total)
    step = 1
    while step < length:
        if step > 1:
            total = (total.astype(jnp.float32) + other.astype(jnp.float32)).astype(jnp.bfloat16)
        pairs = [(i * cycle_size + p, (i ^ step) * cycle_size + p) for i in range(length) for p in positions]
        other = lax.ppermute(total, ("samp", "pair"), pairs)
        step *= 2
    return total, other


def whole_gram_kernel(tile, matrix, gram, block, total, arrivals):
    rows, width = matrix.shape[0], matrix.shape[1] // 2

    def read_of(t):
        here = pl.ds(pl.multiple_of(t * tile, tile), tile)
        return pltpu.make_async_copy(matrix.at[here], block.at[here], arrivals.at[t])

    def start(t, carry):
        read_of(t).start()
        return carry

    def add(t, carry):
        read_of(t).wait()
        here = pl.ds(pl.multiple_of(t * tile, tile), tile)
        total[...] += cross(block[here, :width], block[here, width:])
        return carry

    lax.fori_loop(0, rows // tile, start, 0)
    total[...] = jnp.zeros_like(total)
    lax.fori_loop(0, rows // tile, add, 0)
    gram[...] = total[...].astype(gram.dtype)


def whole_gram(matrix):
    rows, width = matrix.shape[0], matrix.shape[1] // 2
    tile = min(1024, rows)
    return pl.pallas_call(
        functools.partial(whole_gram_kernel, tile),
        out_shape=jax.ShapeDtypeStruct((width, width), matrix.dtype),
        in_specs=[IN_HBM],
        out_specs=IN_VMEM,
        scratch_shapes=[
            pltpu.VMEM(matrix.shape, matrix.dtype),
            pltpu.VMEM((width, width), jnp.float32),
            pltpu.SemaphoreType.DMA((rows // tile,)),
        ],
        compiler_params=pltpu.CompilerParams(vmem_limit_bytes=VMEM_LIMIT),
        cost_estimate=pl.CostEstimate(
            flops=2 * rows * width**2, bytes_accessed=4 * rows * width, transcendentals=0
        ),
    )(matrix)


def cross(first, second):
    return lax.dot_general(
        first, second, (((0,), (0,)), ((), ())), preferred_element_type=jnp.float32
    )


def shards(matrix, tournament):
    cycle_size = lax.axis_size("pair")
    half_cycle = cycle_size // 2
    position = lax.axis_index("pair")
    rows, width = matrix.shape[0], matrix.shape[1] // 2
    half = rows // 2

    def target(p):
        return (p + half_cycle + 1) % cycle_size

    def among(positions):
        found = sum((position == p).astype(jnp.int32) for p in positions)
        return found.reshape((1,))

    def passed(value, pairs):
        return lax.ppermute(value, "pair", pairs)

    def selector(tourney):
        slot_index = (position + half_cycle * (tourney % 2)) % cycle_size
        return lax.dynamic_slice(tournament[tourney], (slot_index,), (1,))

    def sends(positions):
        return [(p, target(p)) for p in positions]

    whole = list(range(cycle_size))
    late = [half_cycle - 1, cycle_size - 1]
    to_late = [p for p in whole if target(p) in late]
    others = [p for p in whole if p not in to_late]
    prompt = [p for p in whole if p not in late]
    late_ways = [
        (cycle_size - 2, half_cycle, cycle_size - 1, half_cycle - 1),
        (half_cycle - 2, half_cycle - 2, half_cycle - 1, cycle_size - 1),
    ]
    ways = [(0, half_cycle - 1, target(0)), (cycle_size - 2, half_cycle + 1, half_cycle - 1)]
    detoured = [source for source, _, _ in ways]
    straight = [p for p in prompt if p not in detoured]
    is_late = among(late)[0] == 1
    after_late = among([target(p) for p in late])
    after_detoured = among([target(p) for p in detoured])

    gram = whole_gram(matrix)
    keeping, first, last = rotation_of(
        selector(0), summed(gram, whole), [[matrix], [matrix]], [[0], [half]], half, [IN_HBM] * 2
    )
    got_first = passed(first, sends(others) + [(source, by) for source, _, by, _ in late_ways])
    got_last = passed(last, sends(others))
    relayed = passed(last, [(source, by) for source, by, _, _ in late_ways])
    kept = rotated_rows([matrix], [0], rows, keeping, [IN_HBM])
    got_first, got_last, relayed = lax.optimization_barrier((got_first, got_last, relayed))
    late_first = passed(got_first, [(by, end) for _, _, by, end in late_ways])
    late_last = passed(relayed, [(by, end) for _, by, _, end in late_ways])

    both = [IN_HBM, ANYWHERE]

    def terms_of(first_half, last_half, positions):
        gram = cross(kept[:half], first_half) + cross(kept[half:], last_half)
        return summed(gram, positions)

    def slot_moved(first_half, last_half, terms):
        return rotation_of(
            selector(1),
            terms,
            [[kept, first_half], [kept, last_half]],
            [[0, 0], [half, 0]],
            half,
            both * 2,
        )

    prompt_keeping, first, last = slot_moved(got_first, got_last, terms_of(got_first, got_last, prompt))
    first, last, late_first, late_last, token = lax.optimization_barrier(
        (first, last, late_first, late_last, jnp.zeros((16, 128), matrix.dtype))
    )
    token = passed(token, [(half_cycle - 2, cycle_size - 2)])
    first, last, late_first, late_last, token = lax.optimization_barrier(
        (first, last, late_first, late_last, token)
    )
    from_first = passed(first, sends(prompt))
    from_last = passed(last, sends(straight) + [(source, by) for source, by, _ in ways])
    from_far = passed(from_last, [(by, end) for _, by, end in ways])

    terms = lax.cond(
        is_late,
        lambda: terms_of(late_first, late_last, late),
        lambda: (jnp.zeros((width, width), matrix.dtype),) * 2,
    )
    late_keeping, first, last = slot_moved(late_first, late_last, terms)
    from_late_first = passed(first, sends(late))
    from_late_last = passed(last, sends(late))

    keeping = jnp.where(is_late, late_keeping, prompt_keeping)
    got_first = jnp.where(is_late, late_first, got_first)
    got_last = jnp.where(is_late, late_last, got_last)
    out = rotated_rows([kept, got_first], [0, 0], half, keeping, both, matrix.shape)
    out = rotated_rows([kept, got_last], [half, 0], half, keeping, both, matrix.shape, out, half)
    out = place((1 - after_late) * (1 - after_detoured), from_last, out, half, [token])
    out = place(1 - after_late, from_first, out, 0)
    out = place(after_late, from_late_first, out, 0)
    out = place(after_late, from_late_last, out, half)
    return place(after_detoured, from_far, out, half)


def solution(mesh):
    placed = (P("samp", "pair"), P())
    return jax.shard_map(
        shards, mesh=mesh, in_specs=placed, out_specs=P("samp", "pair"), check_vma=False
    )
```

```python
import functools

import jax
import jax.numpy as jnp
from jax import lax
from jax.experimental import pallas as pl
from jax.experimental.pallas import tpu as pltpu
from jax.sharding import PartitionSpec as P

POLAR_STEPS = 5
TILE = 2048
VMEM_LIMIT = 48 * 1024 * 1024


coupling = 2.0
start_scale = 6.0

IN_VMEM = pl.BlockSpec(memory_space=pltpu.VMEM)
IN_SMEM = pl.BlockSpec(memory_space=pltpu.SMEM)
ANYWHERE = pl.BlockSpec(memory_space=pl.ANY)
IN_HBM = pl.BlockSpec(memory_space=pltpu.MemorySpace.HBM)


def reads_of(t, sources, starts, tile, block, arrivals):
    rows = pl.multiple_of(t * tile, tile)
    copies, at = [], 0
    for s, (source, start) in enumerate(zip(sources, starts)):
        span = source.shape[1]
        copies.append(
            pltpu.make_async_copy(
                source.at[pl.ds(pl.multiple_of(start + rows, tile), tile)],
                block.at[pl.ds(rows, tile), pl.ds(at, span)],
                arrivals.at[s, t],
            )
        )
        at += span
    return copies


def start_reads(sources, starts, tiles, tile, block, arrivals):
    def start(t, carry):
        for copy in reads_of(t, sources, starts, tile, block, arrivals):
            copy.start()
        return carry

    lax.fori_loop(0, tiles, start, 0)


def write_rotated(sources, starts, tiles, tile, block, arrivals, columns, rotated, out, first_row, departures):
    def write_of(t):
        rows = pl.multiple_of(t * tile, tile)
        return pltpu.make_async_copy(
            rotated.at[pl.ds(rows, tile)],
            out.at[pl.ds(pl.multiple_of(first_row + rows, tile), tile), pl.ds(0, rotated.shape[1])],
            departures.at[t],
        )

    def rotate(t, carry):
        for copy in reads_of(t, sources, starts, tile, block, arrivals):
            copy.wait()
        here = pl.ds(pl.multiple_of(t * tile, tile), tile)
        rotated[here, :] = lax.dot_general(
            block[here, :], columns[...], (((1,), (1,)), ((), ())), preferred_element_type=jnp.float32
        ).astype(rotated.dtype)
        write_of(t).start()
        return carry

    def wait(t, carry):
        write_of(t).wait()
        return carry

    lax.fori_loop(0, tiles, rotate, 0)
    return lambda: lax.fori_loop(0, tiles, wait, 0)


def polar_columns(selector, mine, other, moving, keeping, iterate):
    width = mine.shape[0]
    gram = mine[...].astype(jnp.float32) + other[...].astype(jnp.float32)
    frobenius = jnp.sqrt(jnp.sum(gram * gram, keepdims=True) + 1e-06)
    coupled = coupling * gram / frobenius
    row = lax.broadcasted_iota(jnp.int32, (width, width), 0)
    column = lax.broadcasted_iota(jnp.int32, (width, width), 1)
    diagonal = (row == column).astype(jnp.float32) / start_scale
    iterate[:width, :width] = diagonal
    iterate[width:, width:] = diagonal
    iterate[:width, width:] = coupled / start_scale
    iterate[width:, :width] = -coupled.T / start_scale

    def step(_, carry):
        current = iterate[...]
        rounded = current.astype(jnp.bfloat16)
        square = lax.dot_general(
            rounded, rounded, (((1,), (1,)), ((), ())), preferred_element_type=jnp.float32
        ).astype(jnp.bfloat16)
        iterate[...] = 1.5 * current - 0.5 * jnp.dot(
            square, rounded, preferred_element_type=jnp.float32
        )
        return carry

    lax.fori_loop(0, POLAR_STEPS, step, 0, unroll=True)
    first = iterate[:width, :].astype(jnp.bfloat16)
    second = iterate[width:, :].astype(jnp.bfloat16)
    second_stays = selector[0] == 1

    @pl.when(second_stays)
    def _():
        moving[...] = first
        keeping[...] = second

    @pl.when(jnp.logical_not(second_stays))
    def _():
        moving[...] = second
        keeping[...] = first


def rotation_kernel(tile, starts_of, *refs):
    selector, mine, other = refs[:3]
    counts = [len(starts) for starts in starts_of]
    parts = len(counts)
    tail = refs[3 + sum(counts) :]
    kept_columns, outs = tail[0], tail[1 : 1 + parts]
    iterate, moving, keeping, block, rotated, arrivals, departures, departure = tail[1 + parts :]
    rows = outs[0].shape[0]
    tiles = rows // tile
    at, pieces = 3, []
    for k, count in enumerate(counts):
        here = pl.ds(k * rows, rows)
        pieces.append(
            (refs[at : at + count], starts_of[k], tiles, tile, block.at[here], arrivals.at[k])
        )
        at += count
    for piece in pieces:
        start_reads(*piece)
    polar_columns(selector, mine, other, moving, keeping, iterate)
    waits = [
        write_rotated(
            *piece, moving, rotated.at[pl.ds(k * rows, rows)], outs[k], 0, departures.at[k]
        )
        for k, piece in enumerate(pieces)
    ]
    write = pltpu.make_async_copy(keeping, kept_columns, departure)
    write.start()
    for wait in waits:
        wait()
    write.wait()


def rotation_of(selector, terms, parts, starts_of, rows, where):
    width = terms[0].shape[0]
    tile = min(TILE, rows)
    counts = [len(part) for part in parts]
    columns = (width, 2 * width)
    moved = jax.ShapeDtypeStruct((rows, width), jnp.bfloat16)
    return pl.pallas_call(
        functools.partial(rotation_kernel, tile, starts_of),
        out_shape=[jax.ShapeDtypeStruct(columns, jnp.bfloat16)] + [moved] * len(parts),
        in_specs=[IN_SMEM, IN_VMEM, IN_VMEM] + where,
        out_specs=[IN_HBM] * (1 + len(parts)),
        scratch_shapes=[
            pltpu.VMEM((2 * width, 2 * width), jnp.float32),
            pltpu.VMEM(columns, jnp.bfloat16),
            pltpu.VMEM(columns, jnp.bfloat16),
            pltpu.VMEM((len(parts) * rows, 2 * width), jnp.bfloat16),
            pltpu.VMEM((len(parts) * rows, width), jnp.bfloat16),
            pltpu.SemaphoreType.DMA((len(parts), max(counts), rows // tile)),
            pltpu.SemaphoreType.DMA((len(parts), rows // tile)),
            pltpu.SemaphoreType.DMA(()),
        ],
        compiler_params=pltpu.CompilerParams(vmem_limit_bytes=VMEM_LIMIT),
        cost_estimate=pl.CostEstimate(
            flops=2 * 2 * POLAR_STEPS * (2 * width) ** 3 + 4 * len(parts) * rows * width**2,
            bytes_accessed=10 * width**2 + 6 * len(parts) * rows * width,
            transcendentals=0,
        ),
    )(selector, *terms, *[source for part in parts for source in part])


def rotated_kernel(starts, tile, rows, first_row, *refs):
    columns, sources = refs[0], refs[1 : 1 + len(starts)]
    out, block, rotated, arrivals, departures = refs[-5:]
    tiles = rows // tile
    start_reads(sources, starts, tiles, tile, block, arrivals)
    write_rotated(
        sources, starts, tiles, tile, block, arrivals, columns, rotated, out, first_row, departures
    )()


def rotated_rows(sources, starts, rows, columns, where, shape=None, out=None, first_row=0):
    width = columns.shape[0]
    tile = min(TILE, rows)
    before = [] if out is None else [out]
    return pl.pallas_call(
        functools.partial(rotated_kernel, starts, tile, rows, first_row),
        out_shape=jax.ShapeDtypeStruct(shape or (rows, width), columns.dtype),
        in_specs=[IN_VMEM] + where + [IN_HBM] * len(before),
        out_specs=IN_HBM,
        input_output_aliases={1 + len(sources): 0} if before else {},
        scratch_shapes=[
            pltpu.VMEM((rows, 2 * width), jnp.bfloat16),
            pltpu.VMEM((rows, width), jnp.bfloat16),
            pltpu.SemaphoreType.DMA((len(sources), rows // tile)),
            pltpu.SemaphoreType.DMA((rows // tile,)),
        ],
        compiler_params=pltpu.CompilerParams(vmem_limit_bytes=VMEM_LIMIT),
        cost_estimate=pl.CostEstimate(
            flops=4 * rows * width**2, bytes_accessed=6 * rows * width, transcendentals=0
        ),
    )(columns, *sources, *before)


def place_kernel(tile, first_row, wanted, source, _, *refs):
    out, block, arrivals, departures = refs[-4:]
    rows, width = source.shape

    @pl.when(wanted[0] == 1)
    def _():
        reads = [
            pltpu.make_async_copy(
                source.at[pl.ds(t * tile, tile)], block.at[pl.ds(t * tile, tile)], arrivals.at[t]
            )
            for t in range(rows // tile)
        ]
        writes = [
            pltpu.make_async_copy(
                block.at[pl.ds(t * tile, tile)],
                out.at[pl.ds(first_row + t * tile, tile), pl.ds(width, width)],
                departures.at[t],
            )
            for t in range(rows // tile)
        ]
        for read in reads:
            read.start()
        for read, write in zip(reads, writes):
            read.wait()
            write.start()
        for write in writes:
            write.wait()


def place(wanted, source, out, first_row, after=()):
    rows, width = source.shape
    tile = min(TILE // 4, rows)
    return pl.pallas_call(
        functools.partial(place_kernel, tile, first_row),
        out_shape=jax.ShapeDtypeStruct(out.shape, out.dtype),
        in_specs=[IN_SMEM, ANYWHERE, IN_HBM] + [ANYWHERE] * len(after),
        out_specs=IN_HBM,
        input_output_aliases={2: 0},
        scratch_shapes=[
            pltpu.VMEM((rows, width), jnp.bfloat16),
            pltpu.SemaphoreType.DMA((rows // tile,)),
            pltpu.SemaphoreType.DMA((rows // tile,)),
        ],
        compiler_params=pltpu.CompilerParams(vmem_limit_bytes=VMEM_LIMIT),
        cost_estimate=pl.CostEstimate(flops=0, bytes_accessed=4 * rows * width, transcendentals=0),
    )(wanted, source, out, *after)


def summed(value, positions):
    length, cycle_size = lax.axis_size("samp"), lax.axis_size("pair")
    total = value.astype(jnp.bfloat16)
    if length & (length - 1):
        return lax.psum(total, "samp"), jnp.zeros_like(total)
    other = jnp.zeros_like(total)
    step = 1
    while step < length:
        if step > 1:
            total = (total.astype(jnp.float32) + other.astype(jnp.float32)).astype(jnp.bfloat16)
        pairs = [(i * cycle_size + p, (i ^ step) * cycle_size + p) for i in range(length) for p in positions]
        other = lax.ppermute(total, ("samp", "pair"), pairs)
        step *= 2
    return total, other


def whole_gram_kernel(tile, matrix, gram, block, total, arrivals):
    rows, width = matrix.shape[0], matrix.shape[1] // 2

    def read_of(t):
        here = pl.ds(pl.multiple_of(t * tile, tile), tile)
        return pltpu.make_async_copy(matrix.at[here], block.at[here], arrivals.at[t])

    def start(t, carry):
        read_of(t).start()
        return carry

    def add(t, carry):
        read_of(t).wait()
        here = pl.ds(pl.multiple_of(t * tile, tile), tile)
        total[...] += cross(block[here, :width], block[here, width:])
        return carry

    lax.fori_loop(0, rows // tile, start, 0)
    total[...] = jnp.zeros_like(total)
    lax.fori_loop(0, rows // tile, add, 0)
    gram[...] = total[...].astype(gram.dtype)


def whole_gram(matrix):
    rows, width = matrix.shape[0], matrix.shape[1] // 2
    tile = min(1024, rows)
    return pl.pallas_call(
        functools.partial(whole_gram_kernel, tile),
        out_shape=jax.ShapeDtypeStruct((width, width), matrix.dtype),
        in_specs=[IN_HBM],
        out_specs=IN_VMEM,
        scratch_shapes=[
            pltpu.VMEM(matrix.shape, matrix.dtype),
            pltpu.VMEM((width, width), jnp.float32),
            pltpu.SemaphoreType.DMA((rows // tile,)),
        ],
        compiler_params=pltpu.CompilerParams(vmem_limit_bytes=VMEM_LIMIT),
        cost_estimate=pl.CostEstimate(
            flops=2 * rows * width**2, bytes_accessed=4 * rows * width, transcendentals=0
        ),
    )(matrix)


def cross(first, second):
    return lax.dot_general(
        first, second, (((0,), (0,)), ((), ())), preferred_element_type=jnp.float32
    )


def shards(matrix, tournament):
    cycle_size = lax.axis_size("pair")
    half_cycle = cycle_size // 2
    position = lax.axis_index("pair")
    rows, width = matrix.shape[0], matrix.shape[1] // 2
    half = rows // 2

    def target(p):
        return (p + half_cycle + 1) % cycle_size

    def among(positions):
        found = sum((position == p).astype(jnp.int32) for p in positions)
        return found.reshape((1,))

    def passed(value, pairs):
        return lax.ppermute(value, "pair", pairs)

    def selector(tourney):
        slot_index = (position + half_cycle * (tourney % 2)) % cycle_size
        return lax.dynamic_slice(tournament[tourney], (slot_index,), (1,))

    def sends(positions):
        return [(p, target(p)) for p in positions]

    whole = list(range(cycle_size))
    late = [half_cycle - 1, cycle_size - 1]
    to_late = [p for p in whole if target(p) in late]
    others = [p for p in whole if p not in to_late]
    prompt = [p for p in whole if p not in late]
    late_ways = [
        (cycle_size - 2, half_cycle, cycle_size - 1, half_cycle - 1),
        (half_cycle - 2, half_cycle - 2, half_cycle - 1, cycle_size - 1),
    ]
    ways = [(0, half_cycle - 1, target(0)), (cycle_size - 2, half_cycle + 1, half_cycle - 1)]
    detoured = [source for source, _, _ in ways]
    straight = [p for p in prompt if p not in detoured]
    is_late = among(late)[0] == 1
    after_late = among([target(p) for p in late])
    after_detoured = among([target(p) for p in detoured])

    gram = whole_gram(matrix)
    keeping, first, last = rotation_of(
        selector(0), summed(gram, whole), [[matrix], [matrix]], [[0], [half]], half, [IN_HBM] * 2
    )
    got_first = passed(first, sends(others) + [(source, by) for source, _, by, _ in late_ways])
    got_last = passed(last, sends(others))
    relayed = passed(last, [(source, by) for source, by, _, _ in late_ways])
    kept = rotated_rows([matrix], [0], rows, keeping, [IN_HBM])
    got_first, got_last, relayed = lax.optimization_barrier((got_first, got_last, relayed))
    late_first = passed(got_first, [(by, end) for _, _, by, end in late_ways])
    late_last = passed(relayed, [(by, end) for _, by, _, end in late_ways])

    both = [IN_HBM, ANYWHERE]

    def terms_of(first_half, last_half, positions):
        gram = cross(kept[:half], first_half) + cross(kept[half:], last_half)
        return summed(gram, positions)

    def slot_moved(first_half, last_half, terms):
        return rotation_of(
            selector(1),
            terms,
            [[kept, first_half], [kept, last_half]],
            [[0, 0], [half, 0]],
            half,
            both * 2,
        )

    prompt_keeping, first, last = slot_moved(got_first, got_last, terms_of(got_first, got_last, prompt))
    first, last, late_first, late_last, token = lax.optimization_barrier(
        (first, last, late_first, late_last, jnp.zeros((16, 128), matrix.dtype))
    )
    token = passed(token, [(half_cycle - 2, cycle_size - 2)])
    first, last, late_first, late_last, token = lax.optimization_barrier(
        (first, last, late_first, late_last, token)
    )
    from_first = [passed(first[at : at + half // 2], sends(prompt)) for at in (0, half // 2)]
    from_last = passed(last, sends(straight) + [(source, by) for source, by, _ in ways])
    relays = [(by, end) for _, by, end in ways]
    from_far = [passed(from_last[at : at + half // 2], relays) for at in (0, half // 2)]

    terms = lax.cond(
        is_late,
        lambda: terms_of(late_first, late_last, late),
        lambda: (jnp.zeros((width, width), matrix.dtype),) * 2,
    )
    late_keeping, first, last = slot_moved(late_first, late_last, terms)
    from_late_first = passed(first, sends(late))
    from_late_last = passed(last, sends(late))

    keeping = jnp.where(is_late, late_keeping, prompt_keeping)
    got_first = jnp.where(is_late, late_first, got_first)
    got_last = jnp.where(is_late, late_last, got_last)
    out = rotated_rows([kept, got_first], [0, 0], half, keeping, both, matrix.shape)
    out = rotated_rows([kept, got_last], [half, 0], half, keeping, both, matrix.shape, out, half)
    out = place((1 - after_late) * (1 - after_detoured), from_last, out, half, [token])
    for at, block in zip((0, half // 2), from_first):
        out = place(1 - after_late, block, out, at)
    out = place(after_late, from_late_first, out, 0)
    out = place(after_late, from_late_last, out, half)
    out = place(after_detoured, from_far[0], out, half)
    return place(after_detoured, from_far[1], out, half + half // 2)


def solution(mesh):
    placed = (P("samp", "pair"), P())
    return jax.shard_map(
        shards, mesh=mesh, in_specs=placed, out_specs=P("samp", "pair"), check_vma=False
    )
```

```python
import functools

import jax
import jax.numpy as jnp
from jax import lax
from jax.experimental import pallas as pl
from jax.experimental.pallas import tpu as pltpu
from jax.sharding import PartitionSpec as P

POLAR_STEPS = 5
TILE = 2048
VMEM_LIMIT = 48 * 1024 * 1024


coupling = 2.0
start_scale = 6.0

IN_VMEM = pl.BlockSpec(memory_space=pltpu.VMEM)
IN_SMEM = pl.BlockSpec(memory_space=pltpu.SMEM)
ANYWHERE = pl.BlockSpec(memory_space=pl.ANY)
IN_HBM = pl.BlockSpec(memory_space=pltpu.MemorySpace.HBM)


def reads_of(t, sources, starts, tile, block, arrivals):
    rows = pl.multiple_of(t * tile, tile)
    copies, at = [], 0
    for s, (source, start) in enumerate(zip(sources, starts)):
        span = source.shape[1]
        copies.append(
            pltpu.make_async_copy(
                source.at[pl.ds(pl.multiple_of(start + rows, tile), tile)],
                block.at[pl.ds(rows, tile), pl.ds(at, span)],
                arrivals.at[s, t],
            )
        )
        at += span
    return copies


def start_reads(sources, starts, tiles, tile, block, arrivals):
    def start(t, carry):
        for copy in reads_of(t, sources, starts, tile, block, arrivals):
            copy.start()
        return carry

    lax.fori_loop(0, tiles, start, 0)


def write_rotated(sources, starts, tiles, tile, block, arrivals, columns, rotated, out, first_row, departures):
    def write_of(t):
        rows = pl.multiple_of(t * tile, tile)
        return pltpu.make_async_copy(
            rotated.at[pl.ds(rows, tile)],
            out.at[pl.ds(pl.multiple_of(first_row + rows, tile), tile), pl.ds(0, rotated.shape[1])],
            departures.at[t],
        )

    def rotate(t, carry):
        for copy in reads_of(t, sources, starts, tile, block, arrivals):
            copy.wait()
        here = pl.ds(pl.multiple_of(t * tile, tile), tile)
        rotated[here, :] = lax.dot_general(
            block[here, :], columns[...], (((1,), (1,)), ((), ())), preferred_element_type=jnp.float32
        ).astype(rotated.dtype)
        write_of(t).start()
        return carry

    def wait(t, carry):
        write_of(t).wait()
        return carry

    lax.fori_loop(0, tiles, rotate, 0)
    return lambda: lax.fori_loop(0, tiles, wait, 0)


def polar_columns(selector, mine, other, moving, keeping, iterate):
    width = mine.shape[0]
    gram = mine[...].astype(jnp.float32) + other[...].astype(jnp.float32)
    frobenius = jnp.sqrt(jnp.sum(gram * gram, keepdims=True) + 1e-06)
    coupled = coupling * gram / frobenius
    row = lax.broadcasted_iota(jnp.int32, (width, width), 0)
    column = lax.broadcasted_iota(jnp.int32, (width, width), 1)
    diagonal = (row == column).astype(jnp.float32) / start_scale
    iterate[:width, :width] = diagonal
    iterate[width:, width:] = diagonal
    iterate[:width, width:] = coupled / start_scale
    iterate[width:, :width] = -coupled.T / start_scale

    def step(_, carry):
        current = iterate[...]
        rounded = current.astype(jnp.bfloat16)
        square = lax.dot_general(
            rounded, rounded, (((1,), (1,)), ((), ())), preferred_element_type=jnp.float32
        ).astype(jnp.bfloat16)
        iterate[...] = 1.5 * current - 0.5 * jnp.dot(
            square, rounded, preferred_element_type=jnp.float32
        )
        return carry

    lax.fori_loop(0, POLAR_STEPS, step, 0, unroll=True)
    first = iterate[:width, :].astype(jnp.bfloat16)
    second = iterate[width:, :].astype(jnp.bfloat16)
    second_stays = selector[0] == 1

    @pl.when(second_stays)
    def _():
        moving[...] = first
        keeping[...] = second

    @pl.when(jnp.logical_not(second_stays))
    def _():
        moving[...] = second
        keeping[...] = first


def rotation_kernel(tile, starts_of, *refs):
    selector, mine, other = refs[:3]
    counts = [len(starts) for starts in starts_of]
    parts = len(counts)
    tail = refs[3 + sum(counts) :]
    kept_columns, outs = tail[0], tail[1 : 1 + parts]
    iterate, moving, keeping, block, rotated, arrivals, departures, departure = tail[1 + parts :]
    rows = outs[0].shape[0]
    tiles = rows // tile
    at, pieces = 3, []
    for k, count in enumerate(counts):
        here = pl.ds(k * rows, rows)
        pieces.append(
            (refs[at : at + count], starts_of[k], tiles, tile, block.at[here], arrivals.at[k])
        )
        at += count
    for piece in pieces:
        start_reads(*piece)
    polar_columns(selector, mine, other, moving, keeping, iterate)
    waits = [
        write_rotated(
            *piece, moving, rotated.at[pl.ds(k * rows, rows)], outs[k], 0, departures.at[k]
        )
        for k, piece in enumerate(pieces)
    ]
    write = pltpu.make_async_copy(keeping, kept_columns, departure)
    write.start()
    for wait in waits:
        wait()
    write.wait()


def rotation_of(selector, terms, parts, starts_of, rows, where):
    width = terms[0].shape[0]
    tile = min(TILE, rows)
    counts = [len(part) for part in parts]
    columns = (width, 2 * width)
    moved = jax.ShapeDtypeStruct((rows, width), jnp.bfloat16)
    return pl.pallas_call(
        functools.partial(rotation_kernel, tile, starts_of),
        out_shape=[jax.ShapeDtypeStruct(columns, jnp.bfloat16)] + [moved] * len(parts),
        in_specs=[IN_SMEM, IN_VMEM, IN_VMEM] + where,
        out_specs=[IN_HBM] * (1 + len(parts)),
        scratch_shapes=[
            pltpu.VMEM((2 * width, 2 * width), jnp.float32),
            pltpu.VMEM(columns, jnp.bfloat16),
            pltpu.VMEM(columns, jnp.bfloat16),
            pltpu.VMEM((len(parts) * rows, 2 * width), jnp.bfloat16),
            pltpu.VMEM((len(parts) * rows, width), jnp.bfloat16),
            pltpu.SemaphoreType.DMA((len(parts), max(counts), rows // tile)),
            pltpu.SemaphoreType.DMA((len(parts), rows // tile)),
            pltpu.SemaphoreType.DMA(()),
        ],
        compiler_params=pltpu.CompilerParams(vmem_limit_bytes=VMEM_LIMIT),
        cost_estimate=pl.CostEstimate(
            flops=2 * 2 * POLAR_STEPS * (2 * width) ** 3 + 4 * len(parts) * rows * width**2,
            bytes_accessed=10 * width**2 + 6 * len(parts) * rows * width,
            transcendentals=0,
        ),
    )(selector, *terms, *[source for part in parts for source in part])


def rotated_kernel(starts, tile, rows, first_row, *refs):
    columns, sources = refs[0], refs[1 : 1 + len(starts)]
    out, block, rotated, arrivals, departures = refs[-5:]
    tiles = rows // tile
    start_reads(sources, starts, tiles, tile, block, arrivals)
    write_rotated(
        sources, starts, tiles, tile, block, arrivals, columns, rotated, out, first_row, departures
    )()


def rotated_rows(sources, starts, rows, columns, where, shape=None, out=None, first_row=0):
    width = columns.shape[0]
    tile = min(TILE, rows)
    before = [] if out is None else [out]
    return pl.pallas_call(
        functools.partial(rotated_kernel, starts, tile, rows, first_row),
        out_shape=jax.ShapeDtypeStruct(shape or (rows, width), columns.dtype),
        in_specs=[IN_VMEM] + where + [IN_HBM] * len(before),
        out_specs=IN_HBM,
        input_output_aliases={1 + len(sources): 0} if before else {},
        scratch_shapes=[
            pltpu.VMEM((rows, 2 * width), jnp.bfloat16),
            pltpu.VMEM((rows, width), jnp.bfloat16),
            pltpu.SemaphoreType.DMA((len(sources), rows // tile)),
            pltpu.SemaphoreType.DMA((rows // tile,)),
        ],
        compiler_params=pltpu.CompilerParams(vmem_limit_bytes=VMEM_LIMIT),
        cost_estimate=pl.CostEstimate(
            flops=4 * rows * width**2, bytes_accessed=6 * rows * width, transcendentals=0
        ),
    )(columns, *sources, *before)


def place_kernel(tile, first_row, wanted, source, _, *refs):
    out, block, arrivals, departures = refs[-4:]
    rows, width = source.shape

    @pl.when(wanted[0] == 1)
    def _():
        reads = [
            pltpu.make_async_copy(
                source.at[pl.ds(t * tile, tile)], block.at[pl.ds(t * tile, tile)], arrivals.at[t]
            )
            for t in range(rows // tile)
        ]
        writes = [
            pltpu.make_async_copy(
                block.at[pl.ds(t * tile, tile)],
                out.at[pl.ds(first_row + t * tile, tile), pl.ds(width, width)],
                departures.at[t],
            )
            for t in range(rows // tile)
        ]
        for read in reads:
            read.start()
        for read, write in zip(reads, writes):
            read.wait()
            write.start()
        for write in writes:
            write.wait()


def place(wanted, source, out, first_row, after=()):
    rows, width = source.shape
    tile = min(TILE // 4, rows)
    return pl.pallas_call(
        functools.partial(place_kernel, tile, first_row),
        out_shape=jax.ShapeDtypeStruct(out.shape, out.dtype),
        in_specs=[IN_SMEM, ANYWHERE, IN_HBM] + [ANYWHERE] * len(after),
        out_specs=IN_HBM,
        input_output_aliases={2: 0},
        scratch_shapes=[
            pltpu.VMEM((rows, width), jnp.bfloat16),
            pltpu.SemaphoreType.DMA((rows // tile,)),
            pltpu.SemaphoreType.DMA((rows // tile,)),
        ],
        compiler_params=pltpu.CompilerParams(vmem_limit_bytes=VMEM_LIMIT),
        cost_estimate=pl.CostEstimate(flops=0, bytes_accessed=4 * rows * width, transcendentals=0),
    )(wanted, source, out, *after)


def summed(value, positions):
    length, cycle_size = lax.axis_size("samp"), lax.axis_size("pair")
    total = value.astype(jnp.bfloat16)
    if length & (length - 1):
        return lax.psum(total, "samp"), jnp.zeros_like(total)
    other = jnp.zeros_like(total)
    step = 1
    while step < length:
        if step > 1:
            total = (total.astype(jnp.float32) + other.astype(jnp.float32)).astype(jnp.bfloat16)
        pairs = [(i * cycle_size + p, (i ^ step) * cycle_size + p) for i in range(length) for p in positions]
        other = lax.ppermute(total, ("samp", "pair"), pairs)
        step *= 2
    return total, other


def whole_gram_kernel(tile, matrix, gram, block, total, arrivals):
    rows, width = matrix.shape[0], matrix.shape[1] // 2

    def read_of(t):
        here = pl.ds(pl.multiple_of(t * tile, tile), tile)
        return pltpu.make_async_copy(matrix.at[here], block.at[here], arrivals.at[t])

    def start(t, carry):
        read_of(t).start()
        return carry

    def add(t, carry):
        read_of(t).wait()
        here = pl.ds(pl.multiple_of(t * tile, tile), tile)
        total[...] += cross(block[here, :width], block[here, width:])
        return carry

    lax.fori_loop(0, rows // tile, start, 0)
    total[...] = jnp.zeros_like(total)
    lax.fori_loop(0, rows // tile, add, 0)
    gram[...] = total[...].astype(gram.dtype)


def whole_gram(matrix):
    rows, width = matrix.shape[0], matrix.shape[1] // 2
    tile = min(1024, rows)
    return pl.pallas_call(
        functools.partial(whole_gram_kernel, tile),
        out_shape=jax.ShapeDtypeStruct((width, width), matrix.dtype),
        in_specs=[IN_HBM],
        out_specs=IN_VMEM,
        scratch_shapes=[
            pltpu.VMEM(matrix.shape, matrix.dtype),
            pltpu.VMEM((width, width), jnp.float32),
            pltpu.SemaphoreType.DMA((rows // tile,)),
        ],
        compiler_params=pltpu.CompilerParams(vmem_limit_bytes=VMEM_LIMIT),
        cost_estimate=pl.CostEstimate(
            flops=2 * rows * width**2, bytes_accessed=4 * rows * width, transcendentals=0
        ),
    )(matrix)


def cross(first, second):
    return lax.dot_general(
        first, second, (((0,), (0,)), ((), ())), preferred_element_type=jnp.float32
    )


def shards(matrix, tournament):
    cycle_size = lax.axis_size("pair")
    half_cycle = cycle_size // 2
    position = lax.axis_index("pair")
    rows, width = matrix.shape[0], matrix.shape[1] // 2
    half = rows // 2

    def target(p):
        return (p + half_cycle + 1) % cycle_size

    def among(positions):
        found = sum((position == p).astype(jnp.int32) for p in positions)
        return found.reshape((1,))

    def passed(value, pairs):
        return lax.ppermute(value, "pair", pairs)

    def selector(tourney):
        slot_index = (position + half_cycle * (tourney % 2)) % cycle_size
        return lax.dynamic_slice(tournament[tourney], (slot_index,), (1,))

    def sends(positions):
        return [(p, target(p)) for p in positions]

    whole = list(range(cycle_size))
    late = [half_cycle - 1, cycle_size - 1]
    to_late = [p for p in whole if target(p) in late]
    others = [p for p in whole if p not in to_late]
    prompt = [p for p in whole if p not in late]
    late_ways = [
        (cycle_size - 2, half_cycle, cycle_size - 1, half_cycle - 1),
        (half_cycle - 2, half_cycle - 2, half_cycle - 1, cycle_size - 1),
    ]
    ways = [(0, half_cycle - 1, target(0)), (cycle_size - 2, half_cycle + 1, half_cycle - 1)]
    detoured = [source for source, _, _ in ways]
    straight = [p for p in prompt if p not in detoured]
    is_late = among(late)[0] == 1
    after_late = among([target(p) for p in late])
    after_detoured = among([target(p) for p in detoured])

    gram = whole_gram(matrix)
    keeping, first, last = rotation_of(
        selector(0), summed(gram, whole), [[matrix], [matrix]], [[0], [half]], half, [IN_HBM] * 2
    )
    got_first = passed(first, sends(others) + [(source, by) for source, _, by, _ in late_ways])
    got_last = passed(last, sends(others))
    relayed = passed(last, [(source, by) for source, by, _, _ in late_ways])
    kept = rotated_rows([matrix], [0], rows, keeping, [IN_HBM])
    got_first, got_last, relayed = lax.optimization_barrier((got_first, got_last, relayed))
    late_first = passed(got_first, [(by, end) for _, _, by, end in late_ways])
    late_last = passed(relayed, [(by, end) for _, by, _, end in late_ways])

    both = [IN_HBM, ANYWHERE]

    def terms_of(first_half, last_half, positions):
        gram = cross(kept[:half], first_half) + cross(kept[half:], last_half)
        return summed(gram, positions)

    def slot_moved(first_half, last_half, terms):
        return rotation_of(
            selector(1),
            terms,
            [[kept, first_half], [kept, last_half]],
            [[0, 0], [half, 0]],
            half,
            both * 2,
        )

    prompt_keeping, first, last = slot_moved(got_first, got_last, terms_of(got_first, got_last, prompt))
    first, last, late_first, late_last, token = lax.optimization_barrier(
        (first, last, late_first, late_last, jnp.zeros((16, 128), matrix.dtype))
    )
    token = passed(token, [(half_cycle - 2, cycle_size - 2)])
    first, last, late_first, late_last, token = lax.optimization_barrier(
        (first, last, late_first, late_last, token)
    )
    from_first = [passed(first[: half // 2], sends(prompt)), passed(first[half // 2 :], sends(prompt))]
    from_last = passed(last, sends(straight) + [(source, by) for source, by, _ in ways])
    relays = [(by, end) for _, by, end in ways]
    cuts = ((0, half * 3 // 4), (half * 3 // 4, half))
    from_far = [passed(from_last[a:b], relays) for a, b in cuts]

    terms = lax.cond(
        is_late,
        lambda: terms_of(late_first, late_last, late),
        lambda: (jnp.zeros((width, width), matrix.dtype),) * 2,
    )
    late_keeping, first, last = slot_moved(late_first, late_last, terms)
    from_late_first = passed(first, sends(late))
    from_late_last = passed(last, sends(late))

    keeping = jnp.where(is_late, late_keeping, prompt_keeping)
    got_first = jnp.where(is_late, late_first, got_first)
    got_last = jnp.where(is_late, late_last, got_last)
    out = rotated_rows([kept, got_first], [0, 0], half, keeping, both, matrix.shape)
    out = rotated_rows([kept, got_last], [half, 0], half, keeping, both, matrix.shape, out, half)
    out = place((1 - after_late) * (1 - after_detoured), from_last, out, half, [token])
    for at, block in zip((0, half // 2), from_first):
        out = place(1 - after_late, block, out, at)
    out = place(after_late, from_late_first, out, 0)
    out = place(after_late, from_late_last, out, half)
    out = place(after_detoured, from_far[0], out, half)
    return place(after_detoured, from_far[1], out, half + half * 3 // 4)


def solution(mesh):
    placed = (P("samp", "pair"), P())
    return jax.shard_map(
        shards, mesh=mesh, in_specs=placed, out_specs=P("samp", "pair"), check_vma=False
    )
```
